256 devices in a mesh: dp: 16 (over x, y), mp: 16 (over z, core).
Axes of the slice: x: 4, y: 4, z: 8, core: 2. Of those that a mesh axis runs over, the one named last changes fastest.
Arguments:
- grad_out: bfloat16 [16384, 2560], P(('dp', 'mp')), may hold values from -0.5 to 0.5
- hidden_act: bfloat16 [16384, 13824], P('dp', 'mp'), may hold values from -6 to 6
- carried: bfloat16 [16, 13824, 2560], P('dp', 'mp'), may hold values from -6 to 6
- prior_right: float32 [2560, 64], replicated, may hold values from -6 to 6
Outputs:
- residual_out: bfloat16 [16, 13824, 2560], P('dp', 'mp')
- next_right: float32 [2560, 64], replicated
The draws below stay inside these ranges and needn't reach their ends.
All inputs are finite; a program needn't handle non-finite values.
Results may differ from the reference program's by a relative error of at most 0.0058.
Values may be sent and summed in bfloat16 or wider, within the bound.
No kernel may reach another device: no remote copies, remote signals or barrier semaphores. Data moves between devices by JAX's collectives and lax.ppermute only.
A program may use at most 64 MiB of HBM per device.

```python
import jax
import jax.numpy as jnp
from jax import lax

D = 2560
FF = 13824
RANK = 64
TOK_DEV = 1024
TOKENS = 16384
N_DP = 16


def steps_of(rng, extent, cuts, least, top_value):
    factor_of = 1.0
    for dim, parts in cuts:
        heights = jax.random.uniform(jax.random.fold_in(jax.random.fold_in(rng, 6), dim), (parts,), jnp.float32, least / len(cuts), top_value / len(cuts))
        factor_of = factor_of * jnp.repeat(jnp.exp(heights), extent[dim] // parts).reshape((-1,) + (1,) * (len(extent) - 1 - dim))
    return factor_of


def noise(key, extent, scale, most, cuts=(), kind=jnp.bfloat16):
    loudness = steps_of(key, extent, cuts, -0.22, 0.18) if cuts else 1.0
    array = jax.random.normal(key, extent, jnp.float32) * scale * loudness
    return jnp.minimum(jnp.maximum(array, -most), most).astype(kind)


def setup_inputs(seed: int = 0) -> dict:
    arg_keys = jax.random.split(jax.random.key(seed), 5)
    grad_out = noise(arg_keys[0], (TOKENS, D), (TOK_DEV ** -0.5), 0.5, ((0, 256),))
    hidden_act = noise(arg_keys[1], (TOKENS, FF), 1.0, 6.0, ((0, 16), (1, 16)))
    carried = noise(arg_keys[2], (N_DP, FF, D), 1.0, 6.0, ((0, 16), (1, 16)))
    prior_right = noise(arg_keys[3], (D, RANK), 1.0, 6.0, (), jnp.float32)
    return dict(grad_out=grad_out, hidden_act=hidden_act, carried=carried, prior_right=prior_right)


highest = lax.Precision.HIGHEST
over_rows = (((0,), (0,)), ((), ()))

def ortho_from(gram_matrix, left_rows):
    rank_size = gram_matrix.shape[0]
    identity = jnp.eye(rank_size, dtype=jnp.float32)
    ridge_shift = 0.001 * jnp.trace(gram_matrix) / rank_size
    cholesky_factor = jnp.linalg.cholesky(gram_matrix + ridge_shift * identity)
    inverse = lax.linalg.triangular_solve(cholesky_factor, identity, left_side=True, lower=True)
    return jnp.dot(left_rows.astype(jnp.float32), inverse.T.astype(jnp.float32), precision=highest, preferred_element_type=jnp.float32)

def reference(grad_out, hidden_act, carried, prior_right):

    def merged_of(replica):
        offset = (replica * TOK_DEV).astype(jnp.int32)
        act_rows = lax.dynamic_slice_in_dim(hidden_act, offset, TOK_DEV, 0)
        out_rows = lax.dynamic_slice_in_dim(grad_out, offset, TOK_DEV, 0)
        weight_grad = lax.dot_general(act_rows.astype(jnp.float32), out_rows.astype(jnp.float32), over_rows, preferred_element_type=jnp.float32)
        own = lax.dynamic_index_in_dim(carried, replica, 0, keepdims=False)
        return own.astype(jnp.float32) + weight_grad

    def accumulate(running, replica):
        return (running + merged_of(replica), None)
    replicas = jnp.arange(N_DP, dtype=jnp.int32)
    summed, _ = lax.scan(accumulate, jnp.zeros((FF, D), jnp.float32), replicas)
    left_whole = jnp.dot(summed.astype(jnp.float32), prior_right.astype(jnp.float32), precision=highest, preferred_element_type=jnp.float32)
    gram_matrix = jnp.dot(left_whole.T.astype(jnp.float32), left_whole.astype(jnp.float32), precision=highest, preferred_element_type=jnp.float32)
    ortho_left = ortho_from(gram_matrix, left_whole)
    next_right = lax.dot_general(summed.astype(jnp.float32), ortho_left.astype(jnp.float32), over_rows, precision=highest, preferred_element_type=jnp.float32) / N_DP
    low_rank = jnp.dot(ortho_left.astype(jnp.float32), next_right.T.astype(jnp.float32), precision=highest, preferred_element_type=jnp.float32)
    residual_out = lax.map(lambda replica: (merged_of(replica) - low_rank).astype(jnp.bfloat16), replicas)
    return (residual_out, next_right)
```

```python
import jax
import jax.numpy as jnp
from jax import lax
from jax.sharding import Mesh
from jax.sharding import PartitionSpec as P

MP = ("mp_0", "mp_1")
DP = ("dp_0", "dp_1")
DP_MP = ("dp_0", "dp_1", "mp_0", "mp_1")

bf16 = jnp.bfloat16
f32 = jnp.float32
highest = lax.Precision.HIGHEST


def product(left, right, left_dim, right_dim):
    return lax.dot_general(
        left, right, (((left_dim,), (right_dim,)), ((), ())), preferred_element_type=f32
    )


def sent_to_all(array, axis):
    devices = lax.axis_size(axis)
    return lax.all_to_all(
        jnp.broadcast_to(array[None], (devices, *array.shape)), axis, 0, 0, tiled=True
    )


def halves(array):
    high = lax.reduce_precision(array, 8, 7)
    return high.astype(bf16), (array - high).astype(bf16)


def inverse_factor(gram_matrix):
    rank = gram_matrix.shape[0]
    identity = jnp.eye(rank, dtype=f32)
    shift = 0.001 * jnp.trace(gram_matrix) / rank
    factor = jnp.linalg.cholesky(gram_matrix + shift * identity)
    return lax.linalg.triangular_solve(factor, identity, left_side=True, lower=True)


def per_device(grad_out, hidden_act, carried, prior_right):
    own = carried[0]
    rank = prior_right.shape[1]
    replicas = lax.axis_size(DP)
    rows = own.shape[0] // 2

    gathered = lax.all_gather(grad_out, MP, axis=0, tiled=True)
    prior = jnp.concatenate(halves(prior_right), axis=1)
    proj = product(grad_out, prior, 1, 0)
    proj = jnp.concatenate(halves(proj[:, :rank] + proj[:, rank:]), axis=1)
    proj = sent_to_all(proj, MP).reshape(-1, 2 * rank)
    left = product(own, prior, 1, 0) + product(hidden_act, proj, 0, 0)
    left = left[:, :rank] + left[:, rank:]
    left = jnp.concatenate([left[:rows], left[rows:]], axis=1).astype(bf16)
    left = jnp.sum(sent_to_all(left, DP).astype(f32), axis=0).astype(bf16)
    left = jnp.concatenate([left[:, :rank], left[:, rank:]], axis=0)

    gram = jnp.sum(sent_to_all(product(left, left, 0, 0), MP), axis=0)
    act_left = jnp.concatenate(halves(product(left, hidden_act, 0, 1)), axis=0)
    act_left = product(act_left, gathered, 1, 0)
    right = product(left, own, 0, 0) + act_left[:rank] + act_left[rank:]
    features = right.shape[1] // 4
    right = right.astype(bf16).reshape(4, rank // 4, 4, features)
    right = jnp.swapaxes(right, 1, 2).reshape(16, rank // 4, features)
    right = lax.all_to_all(right, DP, 0, 0, tiled=True)
    right = jnp.sum(right.astype(f32), axis=0).astype(bf16)
    right = jnp.sum(sent_to_all(right, MP).astype(f32), axis=0).astype(bf16)
    right = sent_to_all(right, DP).reshape(4, 4, rank // 4, features)
    right = jnp.swapaxes(right, 1, 2).reshape(rank, 4 * features).astype(f32)

    merged = own.astype(f32) + product(hidden_act, gathered, 0, 0)
    inverse = inverse_factor(gram)
    right = jnp.dot(inverse / replicas, right, precision=highest, preferred_element_type=f32)
    ortho = lax.dot_general(
        left.astype(f32), inverse, (((1,), (1,)), ((), ())), precision=highest,
        preferred_element_type=f32,
    )
    ortho_high, ortho_low = halves(ortho)
    right_high, right_low = halves(right)
    low_rank = product(
        jnp.concatenate([ortho_high, ortho_low, ortho_high], axis=1),
        jnp.concatenate([right_high, right_high, right_low], axis=0),
        1,
        0,
    )
    residual_out = (merged - low_rank).astype(bf16)[None]
    return (residual_out, right.T)


def solution(mesh):
    split = Mesh(mesh.devices.reshape(4, 4, 8, 2), DP_MP)
    placed = (P(DP_MP, None), P(DP, MP), P(DP, MP, None), P())
    return jax.shard_map(
        per_device, mesh=split, in_specs=placed, out_specs=(P(DP, MP, None), P()), check_vma=False
    )
```

```python
import functools

import jax
import jax.numpy as jnp
from jax import lax
from jax.experimental import pallas as pl
from jax.experimental.pallas import tpu as pltpu
from jax.sharding import Mesh
from jax.sharding import PartitionSpec as P

MP = ("mp_0", "mp_1")
DP = ("dp_0", "dp_1")
DP_MP = ("dp_0", "dp_1", "mp_0", "mp_1")

bf16 = jnp.bfloat16
f32 = jnp.float32
highest = lax.Precision.HIGHEST
VMEM = pltpu.VMEM
whole = pl.BlockSpec(memory_space=pltpu.VMEM)
anywhere = pl.BlockSpec(memory_space=pltpu.HBM)
scalars = pl.BlockSpec(memory_space=pltpu.SMEM)
MIB = 1024 * 1024


def product(left, right, left_dim, right_dim):
    return lax.dot_general(
        left, right, (((left_dim,), (right_dim,)), ((), ())), preferred_element_type=f32
    )


def sent(array, axis):
    return lax.all_to_all(array, axis, 0, 0, tiled=True)


def sent_to_all(array, axis):
    devices = lax.axis_size(axis)
    return sent(jnp.broadcast_to(array[None], (devices, *array.shape)), axis)


def halves(array):
    high = lax.reduce_precision(array, 8, 7)
    return high.astype(bf16), (array - high).astype(bf16)


def split(array):
    high = array.astype(bf16)
    return high, (array - high.astype(f32)).astype(bf16)


def call(kernel, out_shape, **options):
    return pl.pallas_call(
        kernel,
        out_shape=out_shape,
        compiler_params=pltpu.CompilerParams(vmem_limit_bytes=48 * MIB),
        **options,
    )


def of(shape, kind):
    return jax.ShapeDtypeStruct(shape, kind)


def left_kernel(parts_ref, own_ref, act_ref, left_ref, gram_ref, right_ref, act_left_ref):
    rows, lanes = left_ref.shape
    rank = lanes // 2
    total = parts_ref[0].astype(f32)
    for i in range(1, parts_ref.shape[0]):
        total = total + parts_ref[i].astype(f32)
    left = total.astype(bf16)
    left_ref[...] = left
    turned = left.astype(f32).T.astype(bf16)
    gram = product(left, left, 0, 0)
    gram = gram[:rank, :rank] + gram[rank:, rank:]
    gram_ref[...] = jnp.concatenate([gram[: rank // 2], gram[rank // 2 :]], axis=1)
    upper, lower = turned[:rank], turned[rank:]
    act_left = product(upper, act_ref[:rows], 1, 0) + product(lower, act_ref[rows:], 1, 0)
    act_left_ref[...] = jnp.concatenate(split(act_left), axis=0)
    right_ref[...] = product(upper, own_ref[:rows], 1, 0) + product(lower, own_ref[rows:], 1, 0)


def chunk_copies(place_ref, chunk_refs, full_ref, sems):
    steps = len(chunk_refs) // 2
    tokens = chunk_refs[0].shape[0]
    copies = []
    for k in range(steps):
        far = lax.rem(place_ref[0] + (steps - k), steps)
        for side in range(2):
            near = place_ref[1] if side == 0 else 1 - place_ref[1]
            row = pl.multiple_of((far * 2 + near) * tokens, tokens)
            i = 2 * k + side
            copies.append(
                pltpu.make_async_copy(
                    chunk_refs[i], full_ref.at[pl.ds(row, tokens), :], sems.at[i]
                )
            )
    return copies


def in_terms(rows):
    high, low = split(rows)
    least = rows - high.astype(f32) - low.astype(f32)
    spare = jnp.zeros((16 - 3 * rows.shape[0], rows.shape[1]), f32)
    return jnp.concatenate([high.astype(f32), low.astype(f32), least, spare], axis=0).astype(bf16)


def from_terms(block):
    return block[0:2] + block[2:4] + block[4:6]


def right_kernel(count, *refs):
    place_ref, act_left_ref, right_ref, gram_ref = refs[:4]
    chunk_refs = refs[4 : 4 + count]
    out_ref, full_ref, sems = refs[4 + count :]
    copies = chunk_copies(place_ref, chunk_refs, full_ref, sems)
    for copy in copies:
        copy.start()
    for copy in copies:
        copy.wait()
    rank = right_ref.shape[0]
    both = product(act_left_ref[...], full_ref[...], 1, 0)
    right = (right_ref[...] + both[:rank] + both[rank:]).astype(bf16)
    height = out_ref.shape[1]
    width = right.shape[1] // 4
    for a in range(4):
        for b in range(4):
            piece = 4 * a + b
            out_ref[piece, :, :width] = right[
                a * height : (a + 1) * height, b * width : (b + 1) * width
            ]
            out_ref[piece, :, width:] = in_terms(gram_ref[2 * piece : 2 * piece + 2, :])


def summed_kernel(parts_ref, out_ref):
    total = parts_ref[0].astype(f32)
    for i in range(1, parts_ref.shape[0]):
        total = total + parts_ref[i].astype(f32)
    width = total.shape[1] - 128
    total = jnp.concatenate(
        [total[:, :width].astype(bf16), in_terms(from_terms(total[:, width:]))], axis=1
    )
    for i in range(out_ref.shape[0]):
        out_ref[i] = total


def merged_kernel(count, *refs):
    place_ref, act_ref, own_ref = refs[:3]
    chunk_refs = refs[3 : 3 + count]
    out_ref, full_ref, sems = refs[3 + count :]
    step = pl.program_id(0)

    @pl.when(step == 0)
    def _():
        copies = chunk_copies(place_ref, chunk_refs, full_ref, sems)
        for copy in copies:
            copy.start()
        for copy in copies:
            copy.wait()

    width = out_ref.shape[1]
    columns = full_ref[:, pl.ds(pl.multiple_of(step * width, width), width)]
    out_ref[...] = own_ref[...].astype(f32) + product(act_ref[...], columns, 1, 0)


def inverse_of(gram):
    rank = gram.shape[0]
    row = lax.broadcasted_iota(jnp.int32, (rank, rank), 0)
    column = lax.broadcasted_iota(jnp.int32, (rank, rank), 1)
    diagonal = row == column
    trace = jnp.sum(jnp.where(diagonal, gram, 0.0), keepdims=True)
    gram = gram + jnp.where(diagonal, 0.001 * (trace / rank), 0.0)
    work = jnp.concatenate([gram, jnp.where(diagonal, 1.0, 0.0)], axis=1)
    rows = lax.broadcasted_iota(jnp.int32, (rank, 1), 0)
    for k in range(rank - 1):
        factor = work[:, k : k + 1] * (1.0 / work[k : k + 1, k : k + 1])
        factor = jnp.where(rows > k, factor, 0.0)
        work = work - factor * work[k : k + 1, :]
    pivots = jnp.sum(jnp.where(diagonal, work[:, :rank], 0.0), axis=1, keepdims=True)
    return work[:, rank:] * lax.rsqrt(pivots)


def residual_kernel(
    replicas, gram_ref, left_ref, right_ref, merged_ref, out_ref, next_ref, ortho_ref, inverse_ref
):
    rows = left_ref.shape[0]
    rank = inverse_ref.shape[0]

    @pl.when(pl.program_id(0) == 0)
    def _():
        gram = jnp.concatenate(
            [from_terms(gram_ref[a, b].astype(f32)) for a in range(4) for b in range(4)], axis=0
        ) * (1.0 / replicas)
        inverse = inverse_of(jnp.concatenate([gram[:, :rank], gram[:, rank:]], axis=0))
        inverse_ref[...] = inverse
        left = left_ref[...]
        high, low = split(inverse)
        least = (inverse - high.astype(f32) - low.astype(f32)).astype(bf16)
        for i in range(2):
            part = left[:, i * rank : (i + 1) * rank]
            ortho = product(part, high, 1, 1) + product(part, low, 1, 1) + product(part, least, 1, 1)
            high_part, low_part = split(ortho)
            ortho_ref[i * rows : (i + 1) * rows, :] = jnp.concatenate(
                [high_part, low_part, high_part], axis=1
            )

    right = jnp.concatenate([right_ref[a, 0] for a in range(4)], axis=0).astype(f32)
    turned = jnp.dot(
        inverse_ref[...], right, precision=highest, preferred_element_type=f32
    ) * (1.0 / replicas)
    next_ref[...] = turned
    high, low = split(turned)
    low_rank = product(ortho_ref[...], jnp.concatenate([high, high, low], axis=0), 1, 0)
    out_ref[...] = (merged_ref[...] - low_rank).astype(bf16)


def ring_of(own):
    size = lax.axis_size("mp_0")
    chunks = {0: own}
    for back in range(1, size // 2 + 1):
        chunks[back] = lax.ppermute(
            chunks[back - 1], "mp_0", [(i, (i + 1) % size) for i in range(size)]
        )
        if back < size // 2:
            chunks[size - back] = lax.ppermute(
                chunks[(size - back + 1) % size], "mp_0", [(i, (i - 1) % size) for i in range(size)]
            )
    both = []
    for k in range(size):
        both += [chunks[k], lax.ppermute(chunks[k], "mp_1", [(0, 1), (1, 0)])]
    return both


def per_device(grad_out, hidden_act, carried, prior_right):
    own = carried[0]
    act = hidden_act.T
    features = own.shape[1]
    rank = prior_right.shape[1]
    replicas = lax.axis_size(DP)
    rows = own.shape[0] // 2
    tokens = hidden_act.shape[0]
    place = jnp.stack([lax.axis_index("mp_0"), lax.axis_index("mp_1")]).astype(jnp.int32)

    prior = jnp.concatenate(halves(prior_right), axis=1)
    proj = product(grad_out, prior, 1, 0)
    proj = jnp.concatenate(halves(proj[:, :rank] + proj[:, rank:]), axis=1)
    proj = sent_to_all(proj, MP).reshape(-1, 2 * rank)
    chunks = ring_of(grad_out)
    proj, chunks[2], chunks[14] = lax.optimization_barrier((proj, chunks[2], chunks[14]))
    left = product(own, prior, 1, 0) + product(hidden_act, proj, 0, 0)
    left = left[:, :rank] + left[:, rank:]
    left = jnp.concatenate([left[:rows], left[rows:]], axis=1).astype(bf16)
    parts = sent_to_all(left, DP)

    left, gram, right, act_left = call(
        left_kernel,
        (
            of((rows, 2 * rank), bf16),
            of((rank // 2, 2 * rank), f32),
            of((rank, features), f32),
            of((2 * rank, tokens), bf16),
        ),
        in_specs=[whole] * 3,
        out_specs=(whole,) * 4,
        name="left_sum",
    )(parts, own, act)

    scratch = [VMEM((tokens, features), bf16), pltpu.SemaphoreType.DMA((len(chunks),))]
    width = features // 4
    right = call(
        functools.partial(right_kernel, len(chunks)),
        of((16, rank // 4, width + 128), bf16),
        in_specs=[scalars, whole, whole, whole] + [anywhere] * len(chunks),
        out_specs=whole,
        scratch_shapes=scratch,
        name="right_product",
    )(place, act_left, right, gram, *chunks)

    merged = call(
        functools.partial(merged_kernel, len(chunks)),
        of(own.shape, f32),
        grid=(4,),
        in_specs=[scalars, whole, pl.BlockSpec((2 * rows, width), lambda j: (0, j))]
        + [anywhere] * len(chunks),
        out_specs=pl.BlockSpec((2 * rows, width), lambda j: (0, j)),
        scratch_shapes=scratch,
        name="merged",
    )(place, act, own, *chunks)

    for axis in (DP, MP):
        right = call(
            summed_kernel,
            of((16, rank // 4, width + 128), bf16),
            in_specs=[whole],
            out_specs=whole,
            name="summed",
        )(sent(right, axis))
    right = sent(right, DP).reshape(4, 4, rank // 4, width + 128)

    residual_out, next_right = call(
        functools.partial(residual_kernel, replicas),
        (of(own.shape, bf16), of((rank, features), f32)),
        grid=(4,),
        in_specs=[
            pl.BlockSpec((4, 4, rank // 4, 128), lambda j: (0, 0, 0, width // 128)),
            pl.BlockSpec((rows, 2 * rank), lambda j: (0, 0)),
            pl.BlockSpec((4, 1, rank // 4, width), lambda j: (0, j, 0, 0)),
            pl.BlockSpec((2 * rows, width), lambda j: (0, j)),
        ],
        out_specs=(
            pl.BlockSpec((2 * rows, width), lambda j: (0, j)),
            pl.BlockSpec((rank, width), lambda j: (0, j)),
        ),
        scratch_shapes=[VMEM((2 * rows, 3 * rank), bf16), VMEM((rank, rank), f32)],
        name="residual",
    )(right, left, right, merged)
    return (residual_out[None], next_right.T)


def solution(mesh):
    parted = Mesh(mesh.devices.reshape(4, 4, 8, 2), DP_MP)
    placed = (P(DP_MP, None), P(DP, MP), P(DP, MP, None), P())
    return jax.shard_map(
        per_device, mesh=parted, in_specs=placed, out_specs=(P(DP, MP, None), P()), check_vma=False
    )
```

```python
import functools

import jax
import jax.numpy as jnp
from jax import lax
from jax.experimental import pallas as pl
from jax.experimental.pallas import tpu as pltpu
from jax.sharding import Mesh
from jax.sharding import PartitionSpec as P

MP = ("mp_0", "mp_1")
DP = ("dp_0", "dp_1")
DP_MP = ("dp_0", "dp_1", "mp_0", "mp_1")

bf16 = jnp.bfloat16
f32 = jnp.float32
highest = lax.Precision.HIGHEST
VMEM = pltpu.VMEM
whole = pl.BlockSpec(memory_space=pltpu.VMEM)
anywhere = pl.BlockSpec(memory_space=pl.ANY)
in_hbm = pl.BlockSpec(memory_space=pltpu.HBM)
scalars = pl.BlockSpec(memory_space=pltpu.SMEM)
MIB = 1024 * 1024


def product(left, right, left_dim, right_dim):
    return lax.dot_general(
        left, right, (((left_dim,), (right_dim,)), ((), ())), preferred_element_type=f32
    )


def sent(array, axis):
    return lax.all_to_all(array, axis, 0, 0, tiled=True)


def sent_to_all(array, axis):
    devices = lax.axis_size(axis)
    return sent(jnp.broadcast_to(array[None], (devices, *array.shape)), axis)


def halves(array):
    high = lax.reduce_precision(array, 8, 7)
    return high.astype(bf16), (array - high).astype(bf16)


def split(array):
    high = array.astype(bf16)
    return high, (array - high.astype(f32)).astype(bf16)


def call(kernel, out_shape, limit=8, **options):
    return pl.pallas_call(
        kernel,
        out_shape=out_shape,
        compiler_params=pltpu.CompilerParams(vmem_limit_bytes=limit * MIB),
        **options,
    )


def of(shape, kind):
    return jax.ShapeDtypeStruct(shape, kind)


def chunk_copies(place_ref, chunk_refs, half_ref, sems):
    steps = len(chunk_refs)
    tokens = chunk_refs[0].shape[0]
    copies = []
    for k, chunk_ref in enumerate(chunk_refs):
        row = lax.rem(place_ref[0] + (steps - k), steps) * tokens
        copies.append(
            pltpu.make_async_copy(
                chunk_ref, half_ref.at[pl.ds(pl.multiple_of(row, tokens), tokens), :], sems.at[k]
            )
        )
    return copies


def in_terms(array):
    high, low = split(array)
    least = (array - high.astype(f32) - low.astype(f32)).astype(bf16)
    return jnp.concatenate([high, low, least], axis=1)


def left_kernel(
    place_ref, parts_ref, act_hbm, own_hbm, left_ref, gram_ref, keep_ref, give_ref, right_ref,
    act_ref, own_ref, sems,
):
    act_copy = pltpu.make_async_copy(act_hbm, act_ref, sems.at[0])
    own_copy = pltpu.make_async_copy(own_hbm, own_ref, sems.at[1])
    act_copy.start()
    own_copy.start()
    rows, lanes = left_ref.shape
    rank = lanes // 2
    left = total_of(parts_ref).astype(bf16)
    left_ref[...] = left
    turned = left.astype(f32).T.astype(bf16)
    gram = product(left, left, 0, 0)
    gram = gram[:rank, :rank] + gram[rank:, rank:]
    gram_ref[...] = jnp.concatenate([gram[: rank // 2], gram[rank // 2 :]], axis=1)
    upper, lower = turned[:rank], turned[rank:]
    act_copy.wait()
    act_left = product(upper, act_ref[:rows], 1, 0) + product(lower, act_ref[rows:], 1, 0)
    act_left = jnp.concatenate(split(act_left.T), axis=1)
    first = place_ref[1] == 0
    tokens = 64
    for z in range(act_left.shape[0] // (2 * tokens)):
        near = act_left[2 * z * tokens : (2 * z + 1) * tokens]
        far = act_left[(2 * z + 1) * tokens : (2 * z + 2) * tokens]
        keep_ref[z * tokens : (z + 1) * tokens, :] = jnp.where(first, near, far)
        give_ref[z * tokens : (z + 1) * tokens, :] = jnp.where(first, far, near)
    own_copy.wait()
    right_ref[...] = product(upper, own_ref[:rows], 1, 0) + product(lower, own_ref[rows:], 1, 0)


def right_kernel(count, *refs):
    place_ref, keep_ref, other_ref, right_ref = refs[:4]
    chunk_refs = refs[4 : 4 + count]
    out_ref, half_hbm, half_ref, sems = refs[4 + count :]
    copies = chunk_copies(place_ref, chunk_refs, half_ref, sems)
    for copy in copies:
        copy.start()
    rank = right_ref.shape[0]
    both = keep_ref[...].astype(f32) + other_ref[...].astype(f32)
    both = jnp.concatenate(split((both[:, :rank] + both[:, rank:]).T), axis=0)
    for copy in copies:
        copy.wait()
    half_copy = pltpu.make_async_copy(half_ref, half_hbm, sems.at[count])
    half_copy.start()
    both = product(both, half_ref[...], 1, 0)
    right = (right_ref[...] + both[:rank] + both[rank:]).astype(bf16)
    height, width = out_ref.shape[1:]
    for a in range(4):
        for b in range(4):
            out_ref[4 * a + b] = right[a * height : (a + 1) * height, b * width : (b + 1) * width]
    half_copy.wait()


def merged_kernel(place_ref, act_ref, own_ref, half_ref, other_ref, out_ref, full_ref):
    tokens = 64
    for z in range(half_ref.shape[0] // tokens):
        rows = slice(z * tokens, (z + 1) * tokens)
        for ref, near in ((half_ref, place_ref[1]), (other_ref, 1 - place_ref[1])):
            row = pl.multiple_of((2 * z + near) * tokens, tokens)
            full_ref[pl.ds(row, tokens), :] = ref[rows, :]
    out_ref[...] = own_ref[...].astype(f32) + product(act_ref[...], full_ref[...], 1, 0)


def total_of(parts_ref):
    total = parts_ref[0].astype(f32)
    for i in range(1, parts_ref.shape[0]):
        total = total + parts_ref[i].astype(f32)
    return total


def replica_sum_kernel(parts_ref, out_ref):
    out_ref[...] = total_of(parts_ref).astype(bf16)


def core_sum_kernel(place_ref, own_ref, other_ref, gram_ref, other_gram_ref, out_ref):
    right = (own_ref[...].astype(f32) + other_ref[...].astype(f32)).astype(bf16)
    gram = gram_ref[...] + other_gram_ref[...]
    height = gram.shape[0] // 2
    gram = jnp.where(place_ref[1] == 0, gram[:height], gram[height:])
    sent_on = jnp.concatenate([right, in_terms(gram)], axis=1)
    for i in range(out_ref.shape[0]):
        out_ref[i] = sent_on


def chip_sum_kernel(parts_ref, out_ref, gram_ref):
    total = total_of(parts_ref)
    width = out_ref.shape[2]
    right = total[:, :width].astype(bf16)
    for i in range(out_ref.shape[0]):
        out_ref[i] = right
    terms = [total[:, width + 128 * i : width + 128 * (i + 1)] for i in range(3)]
    gram_ref[...] = terms[0] + terms[1] + terms[2]


def inverse_of(gram):
    rank = gram.shape[0]
    row = lax.broadcasted_iota(jnp.int32, (rank, rank), 0)
    column = lax.broadcasted_iota(jnp.int32, (rank, rank), 1)
    diagonal = row == column
    trace = jnp.sum(jnp.where(diagonal, gram, 0.0), keepdims=True)
    gram = gram + jnp.where(diagonal, 0.001 * (trace / rank), 0.0)
    work = jnp.concatenate([gram, jnp.where(diagonal, 1.0, 0.0)], axis=1)
    rows = lax.broadcasted_iota(jnp.int32, (rank, 1), 0)
    group = 4
    for first in range(0, rank, group):
        columns = [
            jnp.broadcast_to(work[:, k : k + 1], work.shape) for k in range(first, first + group)
        ]
        lines = [work[k : k + 1, :] for k in range(first, first + group)]
        for i in range(group):
            k = first + i
            factor = columns[i] * (1.0 / columns[i][k : k + 1, :])
            factor = jnp.where(rows > k, factor, 0.0)
            for j in range(i + 1, group):
                columns[j] = columns[j] - factor * columns[j][k : k + 1, :]
                lines[j] = lines[j] - factor[first + j : first + j + 1, :] * lines[i]
            work = work - factor * lines[i]
    pivots = jnp.sum(jnp.where(diagonal, work[:, :rank], 0.0), axis=1, keepdims=True)
    return work[:, rank:] * lax.rsqrt(pivots)


def inverse_kernel(place_ref, gram_ref, other_ref, out_ref):
    own, other = gram_ref[...], other_ref[...]
    first = place_ref[1] == 0
    upper, lower = jnp.where(first, own, other), jnp.where(first, other, own)
    rank = out_ref.shape[0]
    gram = jnp.concatenate([upper[:, :rank], lower[:, :rank], upper[:, rank:], lower[:, rank:]], axis=0)
    out_ref[...] = inverse_of(gram)


def residual_kernel(
    replicas, inverse_ref, left_ref, right_ref, merged_ref, out_ref, next_ref, ortho_ref
):
    rows = left_ref.shape[0]
    rank = inverse_ref.shape[0]

    @pl.when(pl.program_id(0) == 0)
    def _():
        left = left_ref[...]
        inverse = inverse_ref[...]
        high, low = split(inverse)
        least = (inverse - high.astype(f32) - low.astype(f32)).astype(bf16)
        for i in range(2):
            part = left[:, i * rank : (i + 1) * rank]
            ortho = product(part, high, 1, 1) + product(part, low, 1, 1) + product(part, least, 1, 1)
            high_part, low_part = split(ortho)
            ortho_ref[i * rows : (i + 1) * rows, :] = jnp.concatenate(
                [high_part, low_part, high_part], axis=1
            )

    right = jnp.concatenate([right_ref[a, 0] for a in range(4)], axis=0).astype(f32)
    turned = jnp.dot(
        inverse_ref[...], right, precision=highest, preferred_element_type=f32
    ) * (1.0 / replicas)
    next_ref[...] = turned
    high, low = split(turned)
    low_rank = product(ortho_ref[...], jnp.concatenate([high, high, low], axis=0), 1, 0)
    out_ref[...] = (merged_ref[...] - low_rank).astype(bf16)


def swapped(array):
    return lax.ppermute(array, "mp_1", [(0, 1), (1, 0)])


class Ring:
    def __init__(self, own):
        self.size = lax.axis_size("mp_0")
        self.chunks = {0: own}
        self.done = 0

    def passed(self, array, hop):
        return lax.ppermute(
            array, "mp_0", [(i, (i + hop) % self.size) for i in range(self.size)]
        )

    def step(self, later=None):
        size, k = self.size, self.done + 1
        self.chunks[k] = self.passed(self.chunks[k - 1], 1)
        if k < size // 2:
            self.chunks[size - k] = self.passed(self.chunks[(size - k + 1) % size], -1)
        self.done = k
        if later is not None:
            both = (later, self.chunks[k], self.chunks[size - k])
            later, self.chunks[k], self.chunks[size - k] = lax.optimization_barrier(both)
        return later

    def all(self):
        return tuple(self.chunks[k] for k in range(self.size))


def per_device(grad_out, hidden_act, carried, prior_right):
    own = carried[0]
    act = hidden_act.T
    features = own.shape[1]
    rank = prior_right.shape[1]
    replicas = lax.axis_size(DP)
    rows = own.shape[0] // 2
    tokens = hidden_act.shape[0]
    place = jnp.stack([lax.axis_index("mp_0"), lax.axis_index("mp_1")]).astype(jnp.int32)

    prior = jnp.concatenate(halves(prior_right), axis=1)
    proj = product(grad_out, prior, 1, 0)
    proj = jnp.concatenate(halves(proj[:, :rank] + proj[:, rank:]), axis=1)
    proj = sent_to_all(proj, MP).reshape(-1, 2 * rank)
    ring = Ring(grad_out)
    proj = ring.step(proj)
    left = product(own, prior, 1, 0) + product(hidden_act, proj, 0, 0)
    left = left[:, :rank] + left[:, rank:]
    left = jnp.concatenate([left[:rows], left[rows:]], axis=1).astype(bf16)
    parts = sent_to_all(left, DP)
    for _ in range(3):
        ring.step()
    chunks = ring.all()

    width = features // 4
    half = tokens // 2
    left, gram, keep, give, right = call(
        left_kernel,
        (
            of((rows, 2 * rank), bf16),
            of((rank // 2, 2 * rank), f32),
            of((half, 2 * rank), bf16),
            of((half, 2 * rank), bf16),
            of((rank, features), f32),
        ),
        limit=24,
        in_specs=[scalars, whole, in_hbm, in_hbm],
        out_specs=(whole,) * 5,
        scratch_shapes=[
            VMEM(act.shape, bf16),
            VMEM(own.shape, bf16),
            pltpu.SemaphoreType.DMA((2,)),
        ],
        name="left_sum",
    )(place, parts, act, own)

    right, half_out = call(
        functools.partial(right_kernel, len(chunks)),
        (of((16, rank // 4, width), bf16), of((half, features), bf16)),
        limit=16,
        in_specs=[scalars, whole, whole, whole] + [anywhere] * len(chunks),
        out_specs=(whole, in_hbm),
        scratch_shapes=[VMEM((half, features), bf16), pltpu.SemaphoreType.DMA((len(chunks) + 1,))],
        name="right_product",
    )(place, keep, swapped(give), right, *chunks)

    other_half = swapped(half_out)
    other_gram = swapped(gram)
    right = sent(right, DP)
    right, other_half, other_gram = lax.optimization_barrier((right, other_half, other_gram))
    columns = pl.BlockSpec((half, width), lambda j: (0, j))
    merged = call(
        merged_kernel,
        of(own.shape, f32),
        limit=58,
        grid=(4,),
        in_specs=[
            scalars,
            pl.BlockSpec((2 * rows, tokens), lambda j: (0, 0)),
            pl.BlockSpec((2 * rows, width), lambda j: (0, j)),
            columns,
            columns,
        ],
        out_specs=pl.BlockSpec((2 * rows, width), lambda j: (0, j)),
        scratch_shapes=[VMEM((tokens, width), bf16)],
        name="merged",
    )(place, act, own, half_out, other_half)
    right = call(
        replica_sum_kernel,
        of((rank // 4, width), bf16),
        in_specs=[whole],
        out_specs=whole,
        name="replica_sum",
    )(right)
    right = call(
        core_sum_kernel,
        of((8, rank // 4, width + 384), bf16),
        in_specs=[scalars] + [whole] * 4,
        out_specs=whole,
        name="core_sum",
    )(place, right, swapped(right), gram, other_gram)
    right, merged = lax.optimization_barrier((sent(right, "mp_0"), merged))
    right, gram = call(
        chip_sum_kernel,
        (of((16, rank // 4, width), bf16), of((rank // 4, 2 * rank), f32)),
        in_specs=[whole],
        out_specs=(whole, whole),
        name="chip_sum",
    )(right)
    right = sent(right, DP)
    inverse = call(
        inverse_kernel,
        of((rank, rank), f32),
        in_specs=[scalars, whole, whole],
        out_specs=whole,
        name="inverse",
    )(place, gram, swapped(gram))
    right = right.reshape(4, 4, rank // 4, width)

    residual_out, next_right = call(
        functools.partial(residual_kernel, replicas),
        (of(own.shape, bf16), of((rank, features), f32)),
        limit=58,
        grid=(4,),
        in_specs=[
            pl.BlockSpec((rank, rank), lambda j: (0, 0)),
            pl.BlockSpec((rows, 2 * rank), lambda j: (0, 0)),
            pl.BlockSpec((4, 1, rank // 4, width), lambda j: (0, j, 0, 0)),
            pl.BlockSpec((2 * rows, width), lambda j: (0, j)),
        ],
        out_specs=(
            pl.BlockSpec((2 * rows, width), lambda j: (0, j)),
            pl.BlockSpec((rank, width), lambda j: (0, j)),
        ),
        scratch_shapes=[VMEM((2 * rows, 3 * rank), bf16)],
        name="residual",
    )(inverse, left, right, merged)
    return (residual_out[None], next_right.T)


def solution(mesh):
    parted = Mesh(mesh.devices.reshape(4, 4, 8, 2), DP_MP)
    placed = (P(DP_MP, None), P(DP, MP), P(DP, MP, None), P())
    return jax.shard_map(
        per_device, mesh=parted, in_specs=placed, out_specs=(P(DP, MP, None), P()), check_vma=False
    )
```

```python
import functools

import jax
import jax.numpy as jnp
from jax import lax
from jax.experimental import pallas as pl
from jax.experimental.pallas import tpu as pltpu
from jax.sharding import Mesh
from jax.sharding import PartitionSpec as P

MP = ("mp_0", "mp_1")
DP = ("dp_0", "dp_1")
DP_MP = ("dp_0", "dp_1", "mp_0", "mp_1")

bf16 = jnp.bfloat16
f32 = jnp.float32
highest = lax.Precision.HIGHEST
VMEM = pltpu.VMEM
whole = pl.BlockSpec(memory_space=pltpu.VMEM)
anywhere = pl.BlockSpec(memory_space=pl.ANY)
in_hbm = pl.BlockSpec(memory_space=pltpu.HBM)
MIB = 1024 * 1024


def product(left, right, left_dim, right_dim):
    return lax.dot_general(
        left, right, (((left_dim,), (right_dim,)), ((), ())), preferred_element_type=f32
    )


def sent(array, axis):
    return lax.all_to_all(array, axis, 0, 0, tiled=True)


def sent_to_all(array, axis):
    devices = lax.axis_size(axis)
    return sent(jnp.broadcast_to(array[None], (devices, *array.shape)), axis)


def halves(array):
    high = lax.reduce_precision(array, 8, 7)
    return high.astype(bf16), (array - high).astype(bf16)


def split(array):
    high = array.astype(bf16)
    return high, (array - high.astype(f32)).astype(bf16)


def call(kernel, out_shape, limit=8, **options):
    return pl.pallas_call(
        kernel,
        out_shape=out_shape,
        compiler_params=pltpu.CompilerParams(vmem_limit_bytes=limit * MIB),
        **options,
    )


def of(shape, kind):
    return jax.ShapeDtypeStruct(shape, kind)


def proj_kernel(grad_ref, prior_ref, out_ref):
    grad = grad_ref[...]
    high, low = split(prior_ref[...])
    proj = jnp.concatenate(split(product(grad, high, 1, 1) + product(grad, low, 1, 1)), axis=1)
    for i in range(out_ref.shape[0]):
        out_ref[i] = proj


def chunk_copies(chunk_refs, half_ref, sems):
    steps = len(chunk_refs)
    tokens = chunk_refs[0].shape[0]
    copies = []
    for k, chunk_ref in enumerate(chunk_refs):
        row = lax.rem(lax.axis_index("mp_0") + (steps - k), steps) * tokens
        copies.append(
            pltpu.make_async_copy(
                chunk_ref, half_ref.at[pl.ds(pl.multiple_of(row, tokens), tokens), :], sems.at[k]
            )
        )
    return copies


def in_terms(array):
    high, low = split(array)
    least = (array - high.astype(f32) - low.astype(f32)).astype(bf16)
    return jnp.concatenate([high, low, least], axis=1)


def left_kernel(
    parts_ref, act_hbm, left_ref, turned_ref, gram_ref, keep_ref, give_ref, act_ref, sem
):
    act_copy = pltpu.make_async_copy(act_hbm, act_ref, sem)
    act_copy.start()
    rows, lanes = left_ref.shape
    rank = lanes // 2
    left = total_of(parts_ref).astype(bf16)
    left_ref[...] = left
    turned = left.astype(f32).T.astype(bf16)
    gram = product(left, left, 0, 0)
    gram = gram[:rank, :rank] + gram[rank:, rank:]
    gram_ref[...] = jnp.concatenate([gram[: rank // 2], gram[rank // 2 :]], axis=1)
    upper, lower = turned[:rank], turned[rank:]
    act_copy.wait()
    act_left = product(upper, act_ref[:rows], 1, 0) + product(lower, act_ref[rows:], 1, 0)
    act_left = jnp.concatenate(split(act_left.T), axis=1)
    first = lax.axis_index("mp_1") == 0
    tokens = 64
    for z in range(act_left.shape[0] // (2 * tokens)):
        near = act_left[2 * z * tokens : (2 * z + 1) * tokens]
        far = act_left[(2 * z + 1) * tokens : (2 * z + 2) * tokens]
        keep_ref[z * tokens : (z + 1) * tokens, :] = jnp.where(first, near, far)
        give_ref[z * tokens : (z + 1) * tokens, :] = jnp.where(first, far, near)
    turned_ref[...] = turned


def own_kernel(turned_ref, own_hbm, right_ref, own_ref, sems):
    features = own_ref.shape[1]
    rows = turned_ref.shape[1]
    rank = turned_ref.shape[0] // 2
    width = features // 4
    copies = []
    for b in range(4):
        columns = pl.ds(b * width, width)
        copies.append(
            pltpu.make_async_copy(own_hbm.at[:, columns], own_ref.at[:, columns], sems.at[b])
        )
        copies[b].start()
    turned = turned_ref[...]
    for b in range(4):
        columns = slice(b * width, (b + 1) * width)
        copies[b].wait()
        right_ref[:, columns] = product(turned[:rank], own_ref[:rows, columns], 1, 0) + product(
            turned[rank:], own_ref[rows:, columns], 1, 0
        )


def right_kernel(count, *refs):
    keep_ref, other_ref, right_ref = refs[:3]
    chunk_refs = refs[3 : 3 + count]
    out_ref, half_hbm, half_ref, sems = refs[3 + count :]
    copies = chunk_copies(chunk_refs, half_ref, sems)
    for copy in copies:
        copy.start()
    rank = right_ref.shape[0]
    both = keep_ref[...].astype(f32) + other_ref[...].astype(f32)
    both = jnp.concatenate(split((both[:, :rank] + both[:, rank:]).T), axis=0)
    for copy in copies:
        copy.wait()
    half_copy = pltpu.make_async_copy(half_ref, half_hbm, sems.at[count])
    half_copy.start()
    both = product(both, half_ref[...], 1, 0)
    right = (right_ref[...] + both[:rank] + both[rank:]).astype(bf16)
    height, width = out_ref.shape[1:]
    for a in range(4):
        for b in range(4):
            out_ref[4 * a + b] = right[a * height : (a + 1) * height, b * width : (b + 1) * width]
    half_copy.wait()


def merged_kernel(act_ref, own_ref, half_ref, other_ref, out_ref, full_ref):
    tokens = 64
    for z in range(half_ref.shape[0] // tokens):
        rows = slice(z * tokens, (z + 1) * tokens)
        for ref, near in ((half_ref, lax.axis_index("mp_1")), (other_ref, 1 - lax.axis_index("mp_1"))):
            row = pl.multiple_of((2 * z + near) * tokens, tokens)
            full_ref[pl.ds(row, tokens), :] = ref[rows, :]
    merged = own_ref[...].astype(f32) + product(act_ref[...], full_ref[...], 1, 0)
    out_ref[...] = merged.astype(bf16)


def total_of(parts_ref):
    total = parts_ref[0].astype(f32)
    for i in range(1, parts_ref.shape[0]):
        total = total + parts_ref[i].astype(f32)
    return total


def replica_sum_kernel(parts_ref, out_ref):
    out_ref[...] = total_of(parts_ref).astype(bf16)


def core_sum_kernel(own_ref, other_ref, gram_ref, other_gram_ref, out_ref):
    right = (own_ref[...].astype(f32) + other_ref[...].astype(f32)).astype(bf16)
    gram = gram_ref[...] + other_gram_ref[...]
    height = gram.shape[0] // 2
    gram = jnp.where(lax.axis_index("mp_1") == 0, gram[:height], gram[height:])
    sent_on = jnp.concatenate([right, in_terms(gram)], axis=1)
    for i in range(out_ref.shape[0]):
        out_ref[i] = sent_on


def chip_sum_kernel(parts_ref, out_ref, gram_ref):
    total = total_of(parts_ref)
    width = out_ref.shape[2]
    right = total[:, :width].astype(bf16)
    for i in range(out_ref.shape[0]):
        out_ref[i] = right
    terms = [total[:, width + 128 * i : width + 128 * (i + 1)] for i in range(3)]
    gram_ref[...] = terms[0] + terms[1] + terms[2]


def inverse_of(gram):
    rank = gram.shape[0]
    row = lax.broadcasted_iota(jnp.int32, (rank, rank), 0)
    column = lax.broadcasted_iota(jnp.int32, (rank, rank), 1)
    diagonal = row == column
    trace = jnp.sum(jnp.where(diagonal, gram, 0.0), keepdims=True)
    gram = gram + jnp.where(diagonal, 0.001 * (trace / rank), 0.0)
    work = jnp.concatenate([gram, jnp.where(diagonal, 1.0, 0.0)], axis=1)
    rows = lax.broadcasted_iota(jnp.int32, (rank, 1), 0)
    group = 4
    for first in range(0, rank, group):
        columns = [
            jnp.broadcast_to(work[:, k : k + 1], work.shape) for k in range(first, first + group)
        ]
        lines = [work[k : k + 1, :] for k in range(first, first + group)]
        for i in range(group):
            k = first + i
            factor = columns[i] * (1.0 / columns[i][k : k + 1, :])
            factor = jnp.where(rows > k, factor, 0.0)
            for j in range(i + 1, group):
                columns[j] = columns[j] - factor * columns[j][k : k + 1, :]
                lines[j] = lines[j] - factor[first + j : first + j + 1, :] * lines[i]
            work = work - factor * lines[i]
    pivots = jnp.sum(jnp.where(diagonal, work[:, :rank], 0.0), axis=1, keepdims=True)
    return work[:, rank:] * lax.rsqrt(pivots)


def inverse_kernel(gram_ref, other_ref, left_ref, out_ref, ortho_ref):
    own, other = gram_ref[...], other_ref[...]
    first = lax.axis_index("mp_1") == 0
    upper, lower = jnp.where(first, own, other), jnp.where(first, other, own)
    rank = out_ref.shape[0]
    gram = jnp.concatenate([upper[:, :rank], lower[:, :rank], upper[:, rank:], lower[:, rank:]], axis=0)
    inverse = inverse_of(gram)
    out_ref[...] = inverse
    rows = left_ref.shape[0]
    left = left_ref[...]
    high, low = split(inverse)
    least = (inverse - high.astype(f32) - low.astype(f32)).astype(bf16)
    for i in range(2):
        part = left[:, i * rank : (i + 1) * rank]
        ortho = product(part, high, 1, 1) + product(part, low, 1, 1) + product(part, least, 1, 1)
        high_part, low_part = split(ortho)
        ortho_ref[i * rows : (i + 1) * rows, :] = jnp.concatenate(
            [high_part, low_part, high_part], axis=1
        )


def residual_kernel(replicas, inverse_ref, ortho_ref, right_ref, merged_ref, out_ref, next_ref):
    right = jnp.concatenate([right_ref[a, 0] for a in range(4)], axis=0).astype(f32)
    turned = jnp.dot(
        inverse_ref[...], right, precision=highest, preferred_element_type=f32
    ) * (1.0 / replicas)
    next_ref[...] = turned
    high, low = split(turned)
    low_rank = product(ortho_ref[...], jnp.concatenate([high, high, low], axis=0), 1, 0)
    out_ref[...] = (merged_ref[...].astype(f32) - low_rank).astype(bf16)


def swapped(array):
    return lax.ppermute(array, "mp_1", [(0, 1), (1, 0)])


class Ring:
    def __init__(self, own):
        self.size = lax.axis_size("mp_0")
        self.chunks = {0: own}
        self.done = 0

    def passed(self, array, hop):
        return lax.ppermute(
            array, "mp_0", [(i, (i + hop) % self.size) for i in range(self.size)]
        )

    def step(self, later=None):
        size, k = self.size, self.done + 1
        self.chunks[k] = self.passed(self.chunks[k - 1], 1)
        if k < size // 2:
            self.chunks[size - k] = self.passed(self.chunks[(size - k + 1) % size], -1)
        self.done = k
        if later is not None:
            both = (later, self.chunks[k], self.chunks[size - k])
            later, self.chunks[k], self.chunks[size - k] = lax.optimization_barrier(both)
        return later

    def all(self):
        return tuple(self.chunks[k] for k in range(self.size))


def per_device(grad_out, hidden_act, carried, prior_right):
    own = carried[0]
    act = hidden_act.T
    features = own.shape[1]
    rank = prior_right.shape[1]
    replicas = lax.axis_size(DP)
    rows = own.shape[0] // 2
    tokens = hidden_act.shape[0]

    proj = call(
        proj_kernel,
        of((lax.axis_size("mp_0"), grad_out.shape[0], 2 * rank), bf16),
        in_specs=[whole, whole],
        out_specs=whole,
        name="proj",
    )(grad_out, prior_right.T)
    left = product(own, jnp.concatenate(halves(prior_right), axis=1), 1, 0)
    proj, left = lax.optimization_barrier((sent(proj, "mp_0"), left))
    ring = Ring(grad_out)
    proj = ring.step(proj)
    other = swapped(proj)
    first = lax.axis_index("mp_1") == 0
    proj = jnp.stack([jnp.where(first, proj, other), jnp.where(first, other, proj)], axis=1)
    proj = proj.reshape(-1, 2 * rank)
    left = left + product(hidden_act, proj, 0, 0)
    left = left[:, :rank] + left[:, rank:]
    left = jnp.concatenate([left[:rows], left[rows:]], axis=1).astype(bf16)
    parts = sent_to_all(left, DP)
    for _ in range(3):
        ring.step()
    chunks = ring.all()

    width = features // 4
    half = tokens // 2
    left, turned, gram, keep, give = call(
        left_kernel,
        (
            of((rows, 2 * rank), bf16),
            of((2 * rank, rows), bf16),
            of((rank // 2, 2 * rank), f32),
            of((half, 2 * rank), bf16),
            of((half, 2 * rank), bf16),
        ),
        limit=50,
        in_specs=[whole, in_hbm],
        out_specs=(whole,) * 5,
        scratch_shapes=[VMEM(act.shape, bf16), pltpu.SemaphoreType.DMA],
        name="left_sum",
    )(parts, act)
    right = call(
        own_kernel,
        of((rank, features), f32),
        limit=50,
        in_specs=[whole, in_hbm],
        out_specs=whole,
        scratch_shapes=[VMEM(own.shape, bf16), pltpu.SemaphoreType.DMA((4,))],
        name="own_product",
    )(turned, own)

    right, half_out = call(
        functools.partial(right_kernel, len(chunks)),
        (of((16, rank // 4, width), bf16), of((half, features), bf16)),
        limit=50,
        in_specs=[whole, whole, whole] + [anywhere] * len(chunks),
        out_specs=(whole, in_hbm),
        scratch_shapes=[VMEM((half, features), bf16), pltpu.SemaphoreType.DMA((len(chunks) + 1,))],
        name="right_product",
    )(keep, swapped(give), right, *chunks)

    other_half = swapped(half_out)
    other_gram = swapped(gram)
    right = sent(right, DP)
    right, other_half, other_gram = lax.optimization_barrier((right, other_half, other_gram))
    columns = pl.BlockSpec((half, width), lambda j: (0, j))
    merged = call(
        merged_kernel,
        of(own.shape, bf16),
        limit=58,
        grid=(4,),
        in_specs=[
            pl.BlockSpec((2 * rows, tokens), lambda j: (0, 0)),
            pl.BlockSpec((2 * rows, width), lambda j: (0, j)),
            columns,
            columns,
        ],
        out_specs=pl.BlockSpec((2 * rows, width), lambda j: (0, j)),
        scratch_shapes=[VMEM((tokens, width), bf16)],
        name="merged",
    )(act, own, half_out, other_half)
    right = call(
        replica_sum_kernel,
        of((rank // 4, width), bf16),
        in_specs=[whole],
        out_specs=whole,
        name="replica_sum",
    )(right)
    right = call(
        core_sum_kernel,
        of((8, rank // 4, width + 384), bf16),
        in_specs=[whole] * 4,
        out_specs=whole,
        name="core_sum",
    )(right, swapped(right), gram, other_gram)
    right, merged = lax.optimization_barrier((sent(right, "mp_0"), merged))
    right, gram = call(
        chip_sum_kernel,
        (of((16, rank // 4, width), bf16), of((rank // 4, 2 * rank), f32)),
        in_specs=[whole],
        out_specs=(whole, whole),
        name="chip_sum",
    )(right)
    right = sent(right, DP)
    inverse, ortho = call(
        inverse_kernel,
        (of((rank, rank), f32), of((2 * rows, 3 * rank), bf16)),
        in_specs=[whole] * 3,
        out_specs=(whole, whole),
        name="inverse",
    )(gram, swapped(gram), left)
    right = right.reshape(4, 4, rank // 4, width)

    residual_out, next_right = call(
        functools.partial(residual_kernel, replicas),
        (of(own.shape, bf16), of((rank, features), f32)),
        limit=58,
        grid=(4,),
        in_specs=[
            pl.BlockSpec((rank, rank), lambda j: (0, 0)),
            pl.BlockSpec((2 * rows, 3 * rank), lambda j: (0, 0)),
            pl.BlockSpec((4, 1, rank // 4, width), lambda j: (0, j, 0, 0)),
            pl.BlockSpec((2 * rows, width), lambda j: (0, j)),
        ],
        out_specs=(
            pl.BlockSpec((2 * rows, width), lambda j: (0, j)),
            pl.BlockSpec((rank, width), lambda j: (0, j)),
        ),
        name="residual",
    )(inverse, ortho, right, merged)
    return (residual_out[None], next_right.T)


def solution(mesh):
    parted = Mesh(mesh.devices.reshape(4, 4, 8, 2), DP_MP)
    placed = (P(DP_MP, None), P(DP, MP), P(DP, MP, None), P())
    return jax.shard_map(
        per_device, mesh=parted, in_specs=placed, out_specs=(P(DP, MP, None), P()), check_vma=False
    )
```

```python
import functools

import jax
import jax.numpy as jnp
from jax import lax
from jax.experimental import pallas as pl
from jax.experimental.pallas import tpu as pltpu
from jax.sharding import Mesh
from jax.sharding import PartitionSpec as P

MP = ("mp_0", "mp_1")
DP = ("dp_0", "dp_1")
DP_MP = ("dp_0", "dp_1", "mp_0", "mp_1")

bf16 = jnp.bfloat16
f32 = jnp.float32
highest = lax.Precision.HIGHEST
VMEM = pltpu.VMEM
whole = pl.BlockSpec(memory_space=pltpu.VMEM)
anywhere = pl.BlockSpec(memory_space=pl.ANY)
in_hbm = pl.BlockSpec(memory_space=pltpu.HBM)
MIB = 1024 * 1024


def product(left, right, left_dim, right_dim):
    return lax.dot_general(
        left, right, (((left_dim,), (right_dim,)), ((), ())), preferred_element_type=f32
    )


def sent(array, axis):
    return lax.all_to_all(array, axis, 0, 0, tiled=True)


def sent_to_all(array, axis):
    devices = lax.axis_size(axis)
    return sent(jnp.broadcast_to(array[None], (devices, *array.shape)), axis)


def halves(array):
    high = lax.reduce_precision(array, 8, 7)
    return high.astype(bf16), (array - high).astype(bf16)


def split(array):
    high = array.astype(bf16)
    return high, (array - high.astype(f32)).astype(bf16)


def call(kernel, out_shape, limit=8, **options):
    return pl.pallas_call(
        kernel,
        out_shape=out_shape,
        compiler_params=pltpu.CompilerParams(vmem_limit_bytes=limit * MIB),
        **options,
    )


def of(shape, kind):
    return jax.ShapeDtypeStruct(shape, kind)


def proj_kernel(grad_ref, prior_ref, out_ref):
    grad = grad_ref[...]
    high, low = split(prior_ref[...])
    proj = jnp.concatenate(split(product(grad, high, 1, 1) + product(grad, low, 1, 1)), axis=1)
    for i in range(out_ref.shape[0]):
        out_ref[i] = proj


def chunk_copies(chunk_refs, half_ref, sems):
    steps = len(chunk_refs)
    tokens = chunk_refs[0].shape[0]
    copies = []
    for k, chunk_ref in enumerate(chunk_refs):
        row = lax.rem(lax.axis_index("mp_0") + (steps - k), steps) * tokens
        copies.append(
            pltpu.make_async_copy(
                chunk_ref, half_ref.at[pl.ds(pl.multiple_of(row, tokens), tokens), :], sems.at[k]
            )
        )
    return copies


def in_terms(array):
    high, low = split(array)
    least = (array - high.astype(f32) - low.astype(f32)).astype(bf16)
    return jnp.concatenate([high, low, least], axis=1)


def left_kernel(
    parts_ref, act_hbm, left_hbm, turned_ref, gram_ref, keep_ref, give_ref, act_ref, left_ref, sems
):
    act_copy = pltpu.make_async_copy(act_hbm, act_ref, sems.at[0])
    act_copy.start()
    rows, lanes = left_ref.shape
    rank = lanes // 2
    left = total_of(parts_ref).astype(bf16)
    left_ref[...] = left
    left_copy = pltpu.make_async_copy(left_ref, left_hbm, sems.at[1])
    left_copy.start()
    turned = left.astype(f32).T.astype(bf16)
    gram = product(left, left, 0, 0)
    gram = gram[:rank, :rank] + gram[rank:, rank:]
    gram_ref[...] = jnp.concatenate([gram[: rank // 2], gram[rank // 2 :]], axis=1)
    upper, lower = turned[:rank], turned[rank:]
    act_copy.wait()
    act_left = product(upper, act_ref[:rows], 1, 0) + product(lower, act_ref[rows:], 1, 0)
    act_left = jnp.concatenate(split(act_left.T), axis=1)
    first = lax.axis_index("mp_1") == 0
    tokens = 64
    for z in range(act_left.shape[0] // (2 * tokens)):
        near = act_left[2 * z * tokens : (2 * z + 1) * tokens]
        far = act_left[(2 * z + 1) * tokens : (2 * z + 2) * tokens]
        keep_ref[z * tokens : (z + 1) * tokens, :] = jnp.where(first, near, far)
        give_ref[z * tokens : (z + 1) * tokens, :] = jnp.where(first, far, near)
    turned_ref[...] = turned
    left_copy.wait()


def own_kernel(turned_ref, own_hbm, right_ref, own_ref, sems):
    features = own_ref.shape[1]
    rows = turned_ref.shape[1]
    rank = turned_ref.shape[0] // 2
    width = features // 4
    copies = []
    for b in range(4):
        columns = pl.ds(b * width, width)
        copies.append(
            pltpu.make_async_copy(own_hbm.at[:, columns], own_ref.at[:, columns], sems.at[b])
        )
        copies[b].start()
    turned = turned_ref[...]
    for b in range(4):
        columns = slice(b * width, (b + 1) * width)
        copies[b].wait()
        right_ref[:, columns] = product(turned[:rank], own_ref[:rows, columns], 1, 0) + product(
            turned[rank:], own_ref[rows:, columns], 1, 0
        )


def right_kernel(count, *refs):
    keep_ref, other_ref, right_ref = refs[:3]
    chunk_refs = refs[3 : 3 + count]
    out_ref, half_hbm, half_ref, sems = refs[3 + count :]
    copies = chunk_copies(chunk_refs, half_ref, sems)
    for copy in copies:
        copy.start()
    rank = right_ref.shape[0]
    both = keep_ref[...].astype(f32) + other_ref[...].astype(f32)
    both = jnp.concatenate(split((both[:, :rank] + both[:, rank:]).T), axis=0)
    for copy in copies:
        copy.wait()
    half_copy = pltpu.make_async_copy(half_ref, half_hbm, sems.at[count])
    half_copy.start()
    both = product(both, half_ref[...], 1, 0)
    right = (right_ref[...] + both[:rank] + both[rank:]).astype(bf16)
    height, width = out_ref.shape[1:]
    for a in range(4):
        for b in range(4):
            out_ref[4 * a + b] = right[a * height : (a + 1) * height, b * width : (b + 1) * width]
    half_copy.wait()


def merged_kernel(act_ref, own_ref, half_ref, other_ref, out_ref, full_ref):
    tokens = 64
    for z in range(half_ref.shape[0] // tokens):
        rows = slice(z * tokens, (z + 1) * tokens)
        for ref, near in ((half_ref, lax.axis_index("mp_1")), (other_ref, 1 - lax.axis_index("mp_1"))):
            row = pl.multiple_of((2 * z + near) * tokens, tokens)
            full_ref[pl.ds(row, tokens), :] = ref[rows, :]
    merged = own_ref[...].astype(f32) + product(act_ref[...], full_ref[...], 1, 0)
    out_ref[...] = merged.astype(bf16)


def total_of(parts_ref):
    total = parts_ref[0].astype(f32)
    for i in range(1, parts_ref.shape[0]):
        total = total + parts_ref[i].astype(f32)
    return total


def row_sum_kernel(parts_ref, out_ref):
    total = total_of(parts_ref).astype(bf16)
    for i in range(out_ref.shape[0]):
        out_ref[i] = total


def replica_sum_kernel(parts_ref, out_ref):
    out_ref[...] = total_of(parts_ref).astype(bf16)


def core_sum_kernel(own_ref, other_ref, gram_ref, other_gram_ref, out_ref):
    right = (own_ref[...].astype(f32) + other_ref[...].astype(f32)).astype(bf16)
    gram = gram_ref[...] + other_gram_ref[...]
    height = gram.shape[0] // 2
    gram = jnp.where(lax.axis_index("mp_1") == 0, gram[:height], gram[height:])
    sent_on = jnp.concatenate([right, in_terms(gram)], axis=1)
    for i in range(out_ref.shape[0]):
        out_ref[i] = sent_on


def chip_sum_kernel(parts_ref, out_ref, gram_ref):
    total = total_of(parts_ref)
    width = out_ref.shape[2]
    right = total[:, :width].astype(bf16)
    for i in range(out_ref.shape[0]):
        out_ref[i] = right
    terms = [total[:, width + 128 * i : width + 128 * (i + 1)] for i in range(3)]
    gram_ref[...] = terms[0] + terms[1] + terms[2]


def inverse_of(gram):
    rank = gram.shape[0]
    row = lax.broadcasted_iota(jnp.int32, (rank, rank), 0)
    column = lax.broadcasted_iota(jnp.int32, (rank, rank), 1)
    diagonal = row == column
    trace = jnp.sum(jnp.where(diagonal, gram, 0.0), keepdims=True)
    gram = gram + jnp.where(diagonal, 0.001 * (trace / rank), 0.0)
    work = jnp.concatenate([gram, jnp.where(diagonal, 1.0, 0.0)], axis=1)
    rows = lax.broadcasted_iota(jnp.int32, (rank, 1), 0)
    group = 4
    for first in range(0, rank, group):
        columns = [
            jnp.broadcast_to(work[:, k : k + 1], work.shape) for k in range(first, first + group)
        ]
        lines = [work[k : k + 1, :] for k in range(first, first + group)]
        for i in range(group):
            k = first + i
            factor = columns[i] * (1.0 / columns[i][k : k + 1, :])
            factor = jnp.where(rows > k, factor, 0.0)
            for j in range(i + 1, group):
                columns[j] = columns[j] - factor * columns[j][k : k + 1, :]
                lines[j] = lines[j] - factor[first + j : first + j + 1, :] * lines[i]
            work = work - factor * lines[i]
    pivots = jnp.sum(jnp.where(diagonal, work[:, :rank], 0.0), axis=1, keepdims=True)
    return work[:, rank:] * lax.rsqrt(pivots)


def inverse_kernel(gram_ref, other_ref, left_ref, out_ref, ortho_ref):
    own, other = gram_ref[...], other_ref[...]
    first = lax.axis_index("mp_1") == 0
    upper, lower = jnp.where(first, own, other), jnp.where(first, other, own)
    rank = out_ref.shape[0]
    gram = jnp.concatenate([upper[:, :rank], lower[:, :rank], upper[:, rank:], lower[:, rank:]], axis=0)
    inverse = inverse_of(gram)
    out_ref[...] = inverse
    rows = left_ref.shape[0]
    left = left_ref[...]
    high, low = split(inverse)
    least = (inverse - high.astype(f32) - low.astype(f32)).astype(bf16)
    for i in range(2):
        part = left[:, i * rank : (i + 1) * rank]
        ortho = product(part, high, 1, 1) + product(part, low, 1, 1) + product(part, least, 1, 1)
        high_part, low_part = split(ortho)
        ortho_ref[i * rows : (i + 1) * rows, :] = jnp.concatenate(
            [high_part, low_part, high_part], axis=1
        )


def residual_kernel(replicas, inverse_ref, ortho_ref, right_ref, merged_ref, out_ref, next_ref):
    step = pl.program_id(0)
    right = jnp.concatenate([right_ref[a, step] for a in range(4)], axis=0).astype(f32)
    turned = jnp.dot(
        inverse_ref[...], right, precision=highest, preferred_element_type=f32
    ) * (1.0 / replicas)
    next_ref[...] = turned
    high, low = split(turned)
    low_rank = product(ortho_ref[...], jnp.concatenate([high, high, low], axis=0), 1, 0)
    out_ref[...] = (merged_ref[...].astype(f32) - low_rank).astype(bf16)


def swapped(array):
    return lax.ppermute(array, "mp_1", [(0, 1), (1, 0)])


class Ring:
    def __init__(self, own):
        self.size = lax.axis_size("mp_0")
        self.chunks = {0: own}
        self.done = 0

    def passed(self, array, hop):
        return lax.ppermute(
            array, "mp_0", [(i, (i + hop) % self.size) for i in range(self.size)]
        )

    def step(self, later=None):
        size, k = self.size, self.done + 1
        self.chunks[k] = self.passed(self.chunks[k - 1], 1)
        if k < size // 2:
            self.chunks[size - k] = self.passed(self.chunks[(size - k + 1) % size], -1)
        self.done = k
        if later is not None:
            both = (later, self.chunks[k], self.chunks[size - k])
            later, self.chunks[k], self.chunks[size - k] = lax.optimization_barrier(both)
        return later

    def all(self):
        return tuple(self.chunks[k] for k in range(self.size))


def per_device(grad_out, hidden_act, carried, prior_right):
    own = carried[0]
    act = hidden_act.T
    features = own.shape[1]
    rank = prior_right.shape[1]
    replicas = lax.axis_size(DP)
    rows = own.shape[0] // 2
    tokens = hidden_act.shape[0]

    proj = call(
        proj_kernel,
        of((lax.axis_size("mp_0"), grad_out.shape[0], 2 * rank), bf16),
        limit=63,
        in_specs=[whole, whole],
        out_specs=whole,
        name="proj",
    )(grad_out, prior_right.T)
    left = product(own, jnp.concatenate(halves(prior_right), axis=1), 1, 0)
    proj, left = lax.optimization_barrier((sent(proj, "mp_0"), left))
    ring = Ring(grad_out)
    proj = ring.step(proj)
    other = swapped(proj)
    first = lax.axis_index("mp_1") == 0
    proj = jnp.stack([jnp.where(first, proj, other), jnp.where(first, other, proj)], axis=1)
    proj = proj.reshape(-1, 2 * rank)
    left = left + product(hidden_act, proj, 0, 0)
    left = left[:, :rank] + left[:, rank:]
    left = jnp.concatenate([left[:rows], left[rows:]], axis=1).astype(bf16)
    left = call(
        row_sum_kernel,
        of((lax.axis_size("dp_1"), *left.shape), bf16),
        in_specs=[whole],
        out_specs=whole,
        name="row_sum",
    )(sent_to_all(left, "dp_0"))
    parts = sent(left, "dp_1")
    for _ in range(3):
        ring.step()
    chunks = ring.all()

    width = features // 4
    half = tokens // 2
    left, turned, gram, keep, give = call(
        left_kernel,
        (
            of((rows, 2 * rank), bf16),
            of((2 * rank, rows), bf16),
            of((rank // 2, 2 * rank), f32),
            of((half, 2 * rank), bf16),
            of((half, 2 * rank), bf16),
        ),
        limit=50,
        in_specs=[whole, in_hbm],
        out_specs=(in_hbm,) + (whole,) * 4,
        scratch_shapes=[
            VMEM(act.shape, bf16),
            VMEM((rows, 2 * rank), bf16),
            pltpu.SemaphoreType.DMA((2,)),
        ],
        name="left_sum",
    )(parts, act)
    right = call(
        own_kernel,
        of((rank, features), f32),
        limit=50,
        in_specs=[whole, in_hbm],
        out_specs=whole,
        scratch_shapes=[VMEM(own.shape, bf16), pltpu.SemaphoreType.DMA((4,))],
        name="own_product",
    )(turned, own)

    right, half_out = call(
        functools.partial(right_kernel, len(chunks)),
        (of((16, rank // 4, width), bf16), of((half, features), bf16)),
        limit=50,
        in_specs=[whole, whole, whole] + [anywhere] * len(chunks),
        out_specs=(whole, in_hbm),
        scratch_shapes=[VMEM((half, features), bf16), pltpu.SemaphoreType.DMA((len(chunks) + 1,))],
        name="right_product",
    )(keep, swapped(give), right, *chunks)

    other_half = swapped(half_out)
    other_gram = swapped(gram)
    right = sent(right, DP)
    right, other_half, other_gram = lax.optimization_barrier((right, other_half, other_gram))
    columns = pl.BlockSpec((half, width), lambda j: (0, j))
    merged = call(
        merged_kernel,
        of(own.shape, bf16),
        limit=58,
        grid=(4,),
        in_specs=[
            pl.BlockSpec((2 * rows, tokens), lambda j: (0, 0)),
            pl.BlockSpec((2 * rows, width), lambda j: (0, j)),
            columns,
            columns,
        ],
        out_specs=pl.BlockSpec((2 * rows, width), lambda j: (0, j)),
        scratch_shapes=[VMEM((tokens, width), bf16)],
        name="merged",
    )(act, own, half_out, other_half)
    right = call(
        replica_sum_kernel,
        of((rank // 4, width), bf16),
        in_specs=[whole],
        out_specs=whole,
        name="replica_sum",
    )(right)
    right = call(
        core_sum_kernel,
        of((8, rank // 4, width + 384), bf16),
        in_specs=[whole] * 4,
        out_specs=whole,
        name="core_sum",
    )(right, swapped(right), gram, other_gram)
    right, merged = lax.optimization_barrier((sent(right, "mp_0"), merged))
    right, gram = call(
        chip_sum_kernel,
        (of((16, rank // 4, width), bf16), of((rank // 4, 2 * rank), f32)),
        in_specs=[whole],
        out_specs=(whole, whole),
        name="chip_sum",
    )(right)
    right = sent(right, DP)
    inverse, ortho = call(
        inverse_kernel,
        (of((rank, rank), f32), of((2 * rows, 3 * rank), bf16)),
        in_specs=[whole] * 3,
        out_specs=(whole, whole),
        name="inverse",
    )(gram, swapped(gram), left)
    right = right.reshape(4, 4, rank // 4, width)

    residual_out, next_right = call(
        functools.partial(residual_kernel, replicas),
        (of(own.shape, bf16), of((rank, features), f32)),
        limit=58,
        grid=(4,),
        in_specs=[
            whole,
            whole,
            whole,
            pl.BlockSpec((2 * rows, width), lambda j: (0, j)),
        ],
        out_specs=(
            pl.BlockSpec((2 * rows, width), lambda j: (0, j)),
            pl.BlockSpec((rank, width), lambda j: (0, j)),
        ),
        name="residual",
    )(inverse, ortho, right, merged)
    return (residual_out[None], next_right.T)


def solution(mesh):
    parted = Mesh(mesh.devices.reshape(4, 4, 8, 2), DP_MP)
    placed = (P(DP_MP, None), P(DP, MP), P(DP, MP, None), P())
    return jax.shard_map(
        per_device, mesh=parted, in_specs=placed, out_specs=(P(DP, MP, None), P()), check_vma=False
    )
```

```python
import functools

import jax
import jax.numpy as jnp
from jax import lax
from jax.experimental import pallas as pl
from jax.experimental.pallas import tpu as pltpu
from jax.sharding import Mesh
from jax.sharding import PartitionSpec as P

MP = ("mp_0", "mp_1")
DP = ("dp_0", "dp_1")
DP_MP = ("dp_0", "dp_1", "mp_0", "mp_1")

bf16 = jnp.bfloat16
f32 = jnp.float32
VMEM = pltpu.VMEM
whole = pl.BlockSpec(memory_space=pltpu.VMEM)
anywhere = pl.BlockSpec(memory_space=pl.ANY)
in_hbm = pl.BlockSpec(memory_space=pltpu.HBM)
MIB = 1024 * 1024


def product(left, right, left_dim, right_dim):
    return lax.dot_general(
        left, right, (((left_dim,), (right_dim,)), ((), ())), preferred_element_type=f32
    )


def sent(array, axis):
    return lax.all_to_all(array, axis, 0, 0, tiled=True)


def halves(array):
    high = lax.reduce_precision(array, 8, 7)
    return high.astype(bf16), (array - high).astype(bf16)


def split(array):
    high = array.astype(bf16)
    return high, (array - high.astype(f32)).astype(bf16)


def call(kernel, out_shape, limit=8, **options):
    return pl.pallas_call(
        kernel,
        out_shape=out_shape,
        compiler_params=pltpu.CompilerParams(vmem_limit_bytes=limit * MIB),
        **options,
    )


def of(shape, kind):
    return jax.ShapeDtypeStruct(shape, kind)


def proj_kernel(grad_ref, prior_ref, out_ref):
    grad = grad_ref[...]
    high, low = split(prior_ref[...])
    proj = jnp.concatenate(split(product(grad, high, 1, 1) + product(grad, low, 1, 1)), axis=1)
    for i in range(out_ref.shape[0]):
        out_ref[i] = proj


def local_left_kernel(own_ref, other_ref, carried_ref, act_ref, out_ref):
    first = lax.axis_index("mp_1") == 0
    parts = []
    for z in range(own_ref.shape[0]):
        own, other = own_ref[z], other_ref[z]
        parts += [jnp.where(first, own, other), jnp.where(first, other, own)]
    left = carried_ref[...] + product(act_ref[...], jnp.concatenate(parts, axis=0), 1, 0)
    rows, lanes = out_ref.shape[1:]
    left = left[:, : lanes // 2] + left[:, lanes // 2 :]
    left = jnp.concatenate([left[:rows], left[rows:]], axis=1).astype(bf16)
    for i in range(out_ref.shape[0]):
        out_ref[i] = left


def chunk_copies(chunk_refs, half_ref, sems):
    steps = len(chunk_refs)
    tokens = chunk_refs[0].shape[0]
    copies = []
    for k, chunk_ref in enumerate(chunk_refs):
        row = lax.rem(lax.axis_index("mp_0") + (steps - k), steps) * tokens
        copies.append(
            pltpu.make_async_copy(
                chunk_ref, half_ref.at[pl.ds(pl.multiple_of(row, tokens), tokens), :], sems.at[k]
            )
        )
    return copies


def in_terms(array):
    high, low = split(array)
    least = (array - high.astype(f32) - low.astype(f32)).astype(bf16)
    return jnp.concatenate([high, low, least], axis=1)


def left_kernel(
    parts_ref, act_hbm, left_hbm, turned_ref, gram_ref, keep_ref, give_ref, act_ref, left_ref, sems
):
    act_copy = pltpu.make_async_copy(act_hbm, act_ref, sems.at[0])
    act_copy.start()
    rows, lanes = left_ref.shape
    rank = lanes // 2
    left = total_of(parts_ref).astype(bf16)
    left_ref[...] = left
    left_copy = pltpu.make_async_copy(left_ref, left_hbm, sems.at[1])
    left_copy.start()
    turned = left.astype(f32).T.astype(bf16)
    gram = product(left, left, 0, 0)
    gram = gram[:rank, :rank] + gram[rank:, rank:]
    gram_ref[...] = jnp.concatenate([gram[: rank // 2], gram[rank // 2 :]], axis=1)
    upper, lower = turned[:rank], turned[rank:]
    act_copy.wait()
    act_left = product(upper, act_ref[:rows], 1, 0) + product(lower, act_ref[rows:], 1, 0)
    act_left = jnp.concatenate(split(act_left.T), axis=1)
    first = lax.axis_index("mp_1") == 0
    tokens = 64
    for z in range(act_left.shape[0] // (2 * tokens)):
        near = act_left[2 * z * tokens : (2 * z + 1) * tokens]
        far = act_left[(2 * z + 1) * tokens : (2 * z + 2) * tokens]
        keep_ref[z * tokens : (z + 1) * tokens, :] = jnp.where(first, near, far)
        give_ref[z * tokens : (z + 1) * tokens, :] = jnp.where(first, far, near)
    turned_ref[...] = turned
    left_copy.wait()


def own_kernel(turned_ref, own_hbm, right_ref, own_ref, sems):
    features = own_ref.shape[1]
    rows = turned_ref.shape[1]
    rank = turned_ref.shape[0] // 2
    width = features // 4
    copies = []
    for b in range(4):
        columns = pl.ds(b * width, width)
        copies.append(
            pltpu.make_async_copy(own_hbm.at[:, columns], own_ref.at[:, columns], sems.at[b])
        )
        copies[b].start()
    turned = turned_ref[...]
    for b in range(4):
        columns = slice(b * width, (b + 1) * width)
        copies[b].wait()
        right_ref[:, columns] = product(turned[:rank], own_ref[:rows, columns], 1, 0) + product(
            turned[rank:], own_ref[rows:, columns], 1, 0
        )


def right_kernel(count, *refs):
    keep_ref, other_ref, right_ref = refs[:3]
    chunk_refs = refs[3 : 3 + count]
    out_ref, half_hbm, half_ref, sems = refs[3 + count :]
    copies = chunk_copies(chunk_refs, half_ref, sems)
    for copy in copies:
        copy.start()
    rank = right_ref.shape[0]
    both = keep_ref[...].astype(f32) + other_ref[...].astype(f32)
    both = jnp.concatenate(split((both[:, :rank] + both[:, rank:]).T), axis=0)
    for copy in copies:
        copy.wait()
    half_copy = pltpu.make_async_copy(half_ref, half_hbm, sems.at[count])
    half_copy.start()
    both = product(both, half_ref[...], 1, 0)
    right = (right_ref[...] + both[:rank] + both[rank:]).astype(bf16)
    height, width = out_ref.shape[1:]
    for a in range(4):
        for b in range(4):
            out_ref[4 * a + b] = right[a * height : (a + 1) * height, b * width : (b + 1) * width]
    half_copy.wait()


def merged_kernel(act_ref, own_ref, half_ref, other_ref, out_ref, full_ref):
    tokens = 64
    for z in range(half_ref.shape[0] // tokens):
        rows = slice(z * tokens, (z + 1) * tokens)
        for ref, near in ((half_ref, lax.axis_index("mp_1")), (other_ref, 1 - lax.axis_index("mp_1"))):
            row = pl.multiple_of((2 * z + near) * tokens, tokens)
            full_ref[pl.ds(row, tokens), :] = ref[rows, :]
    merged = own_ref[...].astype(f32) + product(act_ref[...], full_ref[...], 1, 0)
    out_ref[...] = merged.astype(bf16)


def total_of(parts_ref):
    total = parts_ref[0].astype(f32)
    for i in range(1, parts_ref.shape[0]):
        total = total + parts_ref[i].astype(f32)
    return total


def row_sum_kernel(parts_ref, out_ref):
    total = total_of(parts_ref).astype(bf16)
    for i in range(out_ref.shape[0]):
        out_ref[i] = total


def replica_sum_kernel(parts_ref, out_ref):
    out_ref[...] = total_of(parts_ref).astype(bf16)


def core_sum_kernel(own_ref, other_ref, gram_ref, other_gram_ref, out_ref):
    right = (own_ref[...].astype(f32) + other_ref[...].astype(f32)).astype(bf16)
    gram = gram_ref[...] + other_gram_ref[...]
    height = gram.shape[0] // 2
    gram = jnp.where(lax.axis_index("mp_1") == 0, gram[:height], gram[height:])
    sent_on = jnp.concatenate([right, in_terms(gram)], axis=1)
    for i in range(out_ref.shape[0]):
        out_ref[i] = sent_on


def chip_sum_kernel(parts_ref, out_ref, gram_ref):
    total = total_of(parts_ref)
    width = out_ref.shape[2]
    right = total[:, :width].astype(bf16)
    for i in range(out_ref.shape[0]):
        out_ref[i] = right
    terms = [total[:, width + 128 * i : width + 128 * (i + 1)] for i in range(3)]
    gram_ref[...] = terms[0] + terms[1] + terms[2]


def inverse_of(gram):
    rank = gram.shape[0]
    row = lax.broadcasted_iota(jnp.int32, (rank, rank), 0)
    column = lax.broadcasted_iota(jnp.int32, (rank, rank), 1)
    diagonal = row == column
    trace = jnp.sum(jnp.where(diagonal, gram, 0.0), keepdims=True)
    gram = gram + jnp.where(diagonal, 0.001 * (trace / rank), 0.0)
    work = jnp.concatenate([gram, jnp.where(diagonal, 1.0, 0.0)], axis=1)
    rows = lax.broadcasted_iota(jnp.int32, (rank, 1), 0)
    group = 4
    for first in range(0, rank, group):
        columns = [
            jnp.broadcast_to(work[:, k : k + 1], work.shape) for k in range(first, first + group)
        ]
        lines = [work[k : k + 1, :] for k in range(first, first + group)]
        for i in range(group):
            k = first + i
            factor = columns[i] * (1.0 / columns[i][k : k + 1, :])
            factor = jnp.where(rows > k, factor, 0.0)
            for j in range(i + 1, group):
                columns[j] = columns[j] - factor * columns[j][k : k + 1, :]
                lines[j] = lines[j] - factor[first + j : first + j + 1, :] * lines[i]
            work = work - factor * lines[i]
    pivots = jnp.sum(jnp.where(diagonal, work[:, :rank], 0.0), axis=1, keepdims=True)
    return work[:, rank:] * lax.rsqrt(pivots)


def inverse_kernel(gram_ref, other_ref, left_ref, terms_ref, ortho_ref):
    own, other = gram_ref[...], other_ref[...]
    first = lax.axis_index("mp_1") == 0
    upper, lower = jnp.where(first, own, other), jnp.where(first, other, own)
    rank = terms_ref.shape[0]
    gram = jnp.concatenate([upper[:, :rank], lower[:, :rank], upper[:, rank:], lower[:, rank:]], axis=0)
    inverse = inverse_of(gram)
    rows = left_ref.shape[0]
    left = left_ref[...]
    high, low = split(inverse)
    least = (inverse - high.astype(f32) - low.astype(f32)).astype(bf16)
    terms_ref[...] = jnp.concatenate([high, low, least], axis=1)
    for i in range(2):
        part = left[:, i * rank : (i + 1) * rank]
        ortho = product(part, high, 1, 1) + product(part, low, 1, 1) + product(part, least, 1, 1)
        high_part, low_part = split(ortho)
        ortho_ref[i * rows : (i + 1) * rows, :] = jnp.concatenate(
            [high_part, low_part, high_part], axis=1
        )


def residual_kernel(replicas, terms_ref, ortho_ref, right_ref, merged_ref, out_ref, next_ref):
    step = pl.program_id(0)
    right = jnp.concatenate([right_ref[a, step] for a in range(4)] * 3, axis=0)
    turned = product(terms_ref[...], right, 1, 0) * (1.0 / replicas)
    next_ref[...] = turned
    high, low = split(turned)
    low_rank = product(ortho_ref[...], jnp.concatenate([high, high, low], axis=0), 1, 0)
    out_ref[...] = (merged_ref[...].astype(f32) - low_rank).astype(bf16)


def swapped(array):
    return lax.ppermute(array, "mp_1", [(0, 1), (1, 0)])


class Ring:
    def __init__(self, own):
        self.size = lax.axis_size("mp_0")
        self.chunks = {0: own}
        self.done = 0

    def passed(self, array, hop):
        return lax.ppermute(
            array, "mp_0", [(i, (i + hop) % self.size) for i in range(self.size)]
        )

    def step(self, later=None):
        size, k = self.size, self.done + 1
        self.chunks[k] = self.passed(self.chunks[k - 1], 1)
        if k < size // 2:
            self.chunks[size - k] = self.passed(self.chunks[(size - k + 1) % size], -1)
        self.done = k
        if later is not None:
            both = (later, self.chunks[k], self.chunks[size - k])
            later, self.chunks[k], self.chunks[size - k] = lax.optimization_barrier(both)
        return later

    def all(self):
        return tuple(self.chunks[k] for k in range(self.size))


def per_device(grad_out, hidden_act, carried, prior_right):
    own = carried[0]
    act = hidden_act.T
    features = own.shape[1]
    rank = prior_right.shape[1]
    replicas = lax.axis_size(DP)
    rows = own.shape[0] // 2
    tokens = hidden_act.shape[0]

    proj = call(
        proj_kernel,
        of((lax.axis_size("mp_0"), grad_out.shape[0], 2 * rank), bf16),
        limit=63,
        in_specs=[whole, whole],
        out_specs=whole,
        name="proj",
    )(grad_out, prior_right.T)
    proj, passed_on = lax.optimization_barrier((proj, grad_out))
    left = product(own, jnp.concatenate(halves(prior_right), axis=1), 1, 0)
    proj, left = lax.optimization_barrier((sent(proj, "mp_0"), left))
    ring = Ring(passed_on)
    proj = ring.step(proj)
    other = swapped(proj)
    left = call(
        local_left_kernel,
        of((lax.axis_size("dp_0"), rows, 2 * rank), bf16),
        limit=24,
        in_specs=[whole] * 4,
        out_specs=whole,
        name="local_left",
    )(proj, other, left, act)
    left = call(
        row_sum_kernel,
        of((lax.axis_size("dp_1"), rows, 2 * rank), bf16),
        in_specs=[whole],
        out_specs=whole,
        name="row_sum",
    )(sent(left, "dp_0"))
    parts = sent(left, "dp_1")
    for _ in range(3):
        ring.step()
    chunks = ring.all()

    width = features // 4
    half = tokens // 2
    left, turned, gram, keep, give = call(
        left_kernel,
        (
            of((rows, 2 * rank), bf16),
            of((2 * rank, rows), bf16),
            of((rank // 2, 2 * rank), f32),
            of((half, 2 * rank), bf16),
            of((half, 2 * rank), bf16),
        ),
        limit=50,
        in_specs=[whole, in_hbm],
        out_specs=(in_hbm,) + (whole,) * 4,
        scratch_shapes=[
            VMEM(act.shape, bf16),
            VMEM((rows, 2 * rank), bf16),
            pltpu.SemaphoreType.DMA((2,)),
        ],
        name="left_sum",
    )(parts, act)
    right = call(
        own_kernel,
        of((rank, features), f32),
        limit=50,
        in_specs=[whole, in_hbm],
        out_specs=whole,
        scratch_shapes=[VMEM(own.shape, bf16), pltpu.SemaphoreType.DMA((4,))],
        name="own_product",
    )(turned, own)

    right, half_out = call(
        functools.partial(right_kernel, len(chunks)),
        (of((16, rank // 4, width), bf16), of((half, features), bf16)),
        limit=50,
        in_specs=[whole, whole, whole] + [anywhere] * len(chunks),
        out_specs=(whole, in_hbm),
        scratch_shapes=[VMEM((half, features), bf16), pltpu.SemaphoreType.DMA((len(chunks) + 1,))],
        name="right_product",
    )(keep, swapped(give), right, *chunks)

    other_half = swapped(half_out)
    other_gram = swapped(gram)
    right = sent(right, DP)
    right, other_half, other_gram = lax.optimization_barrier((right, other_half, other_gram))
    columns = pl.BlockSpec((half, width), lambda j: (0, j))
    merged = call(
        merged_kernel,
        of(own.shape, bf16),
        limit=58,
        grid=(4,),
        in_specs=[
            pl.BlockSpec((2 * rows, tokens), lambda j: (0, 0)),
            pl.BlockSpec((2 * rows, width), lambda j: (0, j)),
            columns,
            columns,
        ],
        out_specs=pl.BlockSpec((2 * rows, width), lambda j: (0, j)),
        scratch_shapes=[VMEM((tokens, width), bf16)],
        name="merged",
    )(act, own, half_out, other_half)
    right = call(
        replica_sum_kernel,
        of((rank // 4, width), bf16),
        in_specs=[whole],
        out_specs=whole,
        name="replica_sum",
    )(right)
    right = call(
        core_sum_kernel,
        of((8, rank // 4, width + 384), bf16),
        in_specs=[whole] * 4,
        out_specs=whole,
        name="core_sum",
    )(right, swapped(right), gram, other_gram)
    right, merged = lax.optimization_barrier((sent(right, "mp_0"), merged))
    right, gram = call(
        chip_sum_kernel,
        (of((16, rank // 4, width), bf16), of((rank // 4, 2 * rank), f32)),
        in_specs=[whole],
        out_specs=(whole, whole),
        name="chip_sum",
    )(right)
    right = sent(right, DP)
    inverse, ortho = call(
        inverse_kernel,
        (of((rank, 3 * rank), bf16), of((2 * rows, 3 * rank), bf16)),
        in_specs=[whole] * 3,
        out_specs=(whole, whole),
        name="inverse",
    )(gram, swapped(gram), left)
    right = right.reshape(4, 4, rank // 4, width)

    residual_out, next_right = call(
        functools.partial(residual_kernel, replicas),
        (of(own.shape, bf16), of((rank, features), f32)),
        limit=52,
        grid=(4,),
        in_specs=[
            whole,
            whole,
            whole,
            pl.BlockSpec((2 * rows, width), lambda j: (0, j)),
        ],
        out_specs=(
            pl.BlockSpec((2 * rows, width), lambda j: (0, j)),
            pl.BlockSpec((rank, width), lambda j: (0, j)),
        ),
        name="residual",
    )(inverse, ortho, right, merged)
    return (residual_out[None], next_right.T)


def solution(mesh):
    parted = Mesh(mesh.devices.reshape(4, 4, 8, 2), DP_MP)
    placed = (P(DP_MP, None), P(DP, MP), P(DP, MP, None), P())
    return jax.shard_map(
        per_device, mesh=parted, in_specs=placed, out_specs=(P(DP, MP, None), P()), check_vma=False
    )
```

```python
import functools

import jax
import jax.numpy as jnp
from jax import lax
from jax.experimental import pallas as pl
from jax.experimental.pallas import tpu as pltpu
from jax.sharding import Mesh
from jax.sharding import PartitionSpec as P

MP = ("mp_0", "mp_1")
DP = ("dp_0", "dp_1")
DP_MP = ("dp_0", "dp_1", "mp_0", "mp_1")

bf16 = jnp.bfloat16
f32 = jnp.float32
VMEM = pltpu.VMEM
whole = pl.BlockSpec(memory_space=pltpu.VMEM)
anywhere = pl.BlockSpec(memory_space=pl.ANY)
in_hbm = pl.BlockSpec(memory_space=pltpu.HBM)
MIB = 1024 * 1024


def product(left, right, left_dim, right_dim):
    return lax.dot_general(
        left, right, (((left_dim,), (right_dim,)), ((), ())), preferred_element_type=f32
    )


def sent(array, axis):
    return lax.all_to_all(array, axis, 0, 0, tiled=True)


def halves(array):
    high = lax.reduce_precision(array, 8, 7)
    return high.astype(bf16), (array - high).astype(bf16)


def split(array):
    high = array.astype(bf16)
    return high, (array - high.astype(f32)).astype(bf16)


def call(kernel, out_shape, limit=8, **options):
    return pl.pallas_call(
        kernel,
        out_shape=out_shape,
        compiler_params=pltpu.CompilerParams(vmem_limit_bytes=limit * MIB),
        **options,
    )


def of(shape, kind):
    return jax.ShapeDtypeStruct(shape, kind)


def proj_kernel(grad_ref, prior_ref, out_ref):
    grad = grad_ref[...]
    high, low = split(prior_ref[...])
    proj = jnp.concatenate(split(product(grad, high, 1, 1) + product(grad, low, 1, 1)), axis=1)
    for i in range(out_ref.shape[0]):
        out_ref[i] = proj


def local_left_kernel(own_ref, other_ref, carried_ref, act_ref, out_ref):
    first = lax.axis_index("mp_1") == 0
    parts = []
    for z in range(own_ref.shape[0]):
        own, other = own_ref[z], other_ref[z]
        parts += [jnp.where(first, own, other), jnp.where(first, other, own)]
    left = carried_ref[...] + product(act_ref[...], jnp.concatenate(parts, axis=0), 1, 0)
    rows, lanes = out_ref.shape[1:]
    left = left[:, : lanes // 2] + left[:, lanes // 2 :]
    left = jnp.concatenate([left[:rows], left[rows:]], axis=1).astype(bf16)
    for i in range(out_ref.shape[0]):
        out_ref[i] = left


def chunk_copies(chunk_refs, half_ref, sems):
    steps = len(chunk_refs)
    tokens = chunk_refs[0].shape[0]
    copies = []
    for k, chunk_ref in enumerate(chunk_refs):
        row = lax.rem(lax.axis_index("mp_0") + (steps - k), steps) * tokens
        copies.append(
            pltpu.make_async_copy(
                chunk_ref, half_ref.at[pl.ds(pl.multiple_of(row, tokens), tokens), :], sems.at[k]
            )
        )
    return copies


def in_terms(array):
    high, low = split(array)
    least = (array - high.astype(f32) - low.astype(f32)).astype(bf16)
    return jnp.concatenate([high, low, least], axis=1)


def left_kernel(
    parts_ref, act_hbm, left_hbm, turned_ref, gram_ref, keep_ref, give_ref, act_ref, left_ref, sems
):
    act_copy = pltpu.make_async_copy(act_hbm, act_ref, sems.at[0])
    act_copy.start()
    rows, lanes = left_ref.shape
    rank = lanes // 2
    left = total_of(parts_ref).astype(bf16)
    left_ref[...] = left
    left_copy = pltpu.make_async_copy(left_ref, left_hbm, sems.at[1])
    left_copy.start()
    turned = left.astype(f32).T.astype(bf16)
    gram = product(left, left, 0, 0)
    gram = gram[:rank, :rank] + gram[rank:, rank:]
    gram_ref[...] = jnp.concatenate([gram[: rank // 2], gram[rank // 2 :]], axis=1)
    upper, lower = turned[:rank], turned[rank:]
    act_copy.wait()
    act_left = product(upper, act_ref[:rows], 1, 0) + product(lower, act_ref[rows:], 1, 0)
    act_left = jnp.concatenate(split(act_left.T), axis=1)
    first = lax.axis_index("mp_1") == 0
    tokens = 64
    for z in range(act_left.shape[0] // (2 * tokens)):
        near = act_left[2 * z * tokens : (2 * z + 1) * tokens]
        far = act_left[(2 * z + 1) * tokens : (2 * z + 2) * tokens]
        keep_ref[z * tokens : (z + 1) * tokens, :] = jnp.where(first, near, far)
        give_ref[z * tokens : (z + 1) * tokens, :] = jnp.where(first, far, near)
    turned_ref[...] = turned
    left_copy.wait()


def own_kernel(turned_ref, own_hbm, right_ref, own_ref, sems):
    features = own_ref.shape[1]
    rows = turned_ref.shape[1]
    rank = turned_ref.shape[0] // 2
    width = features // 4
    copies = []
    for b in range(4):
        columns = pl.ds(b * width, width)
        copies.append(
            pltpu.make_async_copy(own_hbm.at[:, columns], own_ref.at[:, columns], sems.at[b])
        )
        copies[b].start()
    turned = turned_ref[...]
    for b in range(4):
        columns = slice(b * width, (b + 1) * width)
        copies[b].wait()
        right_ref[:, columns] = product(turned[:rank], own_ref[:rows, columns], 1, 0) + product(
            turned[rank:], own_ref[rows:, columns], 1, 0
        )


def right_kernel(count, *refs):
    keep_ref, other_ref, right_ref = refs[:3]
    chunk_refs = refs[3 : 3 + count]
    out_ref, half_hbm, half_ref, sems = refs[3 + count :]
    copies = chunk_copies(chunk_refs, half_ref, sems)
    for copy in copies:
        copy.start()
    rank = right_ref.shape[0]
    both = keep_ref[...].astype(f32) + other_ref[...].astype(f32)
    both = jnp.concatenate(split((both[:, :rank] + both[:, rank:]).T), axis=0)
    tokens = chunk_refs[0].shape[0]
    kept = []
    for i, copy in enumerate(copies):
        copy.wait()
        row = lax.rem(lax.axis_index("mp_0") + (count - i), count) * tokens
        rows = pl.ds(pl.multiple_of(row, tokens), tokens)
        kept.append(
            pltpu.make_async_copy(half_ref.at[rows, :], half_hbm.at[rows, :], sems.at[count + i])
        )
        kept[i].start()
    both = product(both, half_ref[...], 1, 0)
    right = (right_ref[...] + both[:rank] + both[rank:]).astype(bf16)
    height, width = out_ref.shape[1:]
    for a in range(4):
        for b in range(4):
            out_ref[4 * a + b] = right[a * height : (a + 1) * height, b * width : (b + 1) * width]
    for copy in kept:
        copy.wait()


def merged_kernel(act_ref, own_ref, half_ref, other_ref, out_ref, full_ref):
    tokens = 64
    for z in range(half_ref.shape[0] // tokens):
        rows = slice(z * tokens, (z + 1) * tokens)
        for ref, near in ((half_ref, lax.axis_index("mp_1")), (other_ref, 1 - lax.axis_index("mp_1"))):
            row = pl.multiple_of((2 * z + near) * tokens, tokens)
            full_ref[pl.ds(row, tokens), :] = ref[rows, :]
    merged = own_ref[...].astype(f32) + product(act_ref[...], full_ref[...], 1, 0)
    out_ref[...] = merged.astype(bf16)


def total_of(parts_ref):
    total = parts_ref[0].astype(f32)
    for i in range(1, parts_ref.shape[0]):
        total = total + parts_ref[i].astype(f32)
    return total


def row_sum_kernel(parts_ref, out_ref):
    total = total_of(parts_ref).astype(bf16)
    for i in range(out_ref.shape[0]):
        out_ref[i] = total


def replica_sum_kernel(parts_ref, out_ref):
    out_ref[...] = total_of(parts_ref).astype(bf16)


def core_sum_kernel(own_ref, other_ref, gram_ref, other_gram_ref, out_ref):
    right = (own_ref[...].astype(f32) + other_ref[...].astype(f32)).astype(bf16)
    gram = gram_ref[...] + other_gram_ref[...]
    height = gram.shape[0] // 2
    gram = jnp.where(lax.axis_index("mp_1") == 0, gram[:height], gram[height:])
    sent_on = jnp.concatenate([right, in_terms(gram)], axis=1)
    for i in range(out_ref.shape[0]):
        out_ref[i] = sent_on


def chip_sum_kernel(parts_ref, out_ref, gram_ref):
    total = total_of(parts_ref)
    width = out_ref.shape[2]
    right = total[:, :width].astype(bf16)
    for i in range(out_ref.shape[0]):
        out_ref[i] = right
    terms = [total[:, width + 128 * i : width + 128 * (i + 1)] for i in range(3)]
    gram_ref[...] = terms[0] + terms[1] + terms[2]


def inverse_of(gram):
    rank = gram.shape[0]
    row = lax.broadcasted_iota(jnp.int32, (rank, rank), 0)
    column = lax.broadcasted_iota(jnp.int32, (rank, rank), 1)
    diagonal = row == column
    trace = jnp.sum(jnp.where(diagonal, gram, 0.0), keepdims=True)
    gram = gram + jnp.where(diagonal, 0.001 * (trace / rank), 0.0)
    work = jnp.concatenate([gram, jnp.where(diagonal, 1.0, 0.0)], axis=1)
    rows = lax.broadcasted_iota(jnp.int32, (rank, 1), 0)
    group = 4
    for first in range(0, rank, group):
        columns = [
            jnp.broadcast_to(work[:, k : k + 1], work.shape) for k in range(first, first + group)
        ]
        lines = [work[k : k + 1, :] for k in range(first, first + group)]
        for i in range(group):
            k = first + i
            factor = columns[i] * (1.0 / columns[i][k : k + 1, :])
            factor = jnp.where(rows > k, factor, 0.0)
            for j in range(i + 1, group):
                columns[j] = columns[j] - factor * columns[j][k : k + 1, :]
                lines[j] = lines[j] - factor[first + j : first + j + 1, :] * lines[i]
            work = work - factor * lines[i]
    pivots = jnp.sum(jnp.where(diagonal, work[:, :rank], 0.0), axis=1, keepdims=True)
    return work[:, rank:] * lax.rsqrt(pivots)


def inverse_kernel(gram_ref, other_ref, left_ref, terms_ref, ortho_ref):
    own, other = gram_ref[...], other_ref[...]
    first = lax.axis_index("mp_1") == 0
    upper, lower = jnp.where(first, own, other), jnp.where(first, other, own)
    rank = terms_ref.shape[0]
    gram = jnp.concatenate([upper[:, :rank], lower[:, :rank], upper[:, rank:], lower[:, rank:]], axis=0)
    inverse = inverse_of(gram)
    rows = left_ref.shape[0]
    left = left_ref[...]
    high, low = split(inverse)
    least = (inverse - high.astype(f32) - low.astype(f32)).astype(bf16)
    terms_ref[...] = jnp.concatenate([high, low, least], axis=1)
    for i in range(2):
        part = left[:, i * rank : (i + 1) * rank]
        ortho = product(part, high, 1, 1) + product(part, low, 1, 1) + product(part, least, 1, 1)
        high_part, low_part = split(ortho)
        ortho_ref[i * rows : (i + 1) * rows, :] = jnp.concatenate(
            [high_part, low_part, high_part], axis=1
        )


def residual_kernel(replicas, terms_ref, ortho_ref, right_ref, merged_ref, out_ref, next_ref):
    step = pl.program_id(0)
    right = jnp.concatenate([right_ref[a, step] for a in range(4)] * 3, axis=0)
    turned = product(terms_ref[...], right, 1, 0) * (1.0 / replicas)
    next_ref[...] = turned
    high, low = split(turned)
    low_rank = product(ortho_ref[...], jnp.concatenate([high, high, low], axis=0), 1, 0)
    out_ref[...] = (merged_ref[...].astype(f32) - low_rank).astype(bf16)


def swapped(array):
    return lax.ppermute(array, "mp_1", [(0, 1), (1, 0)])


class Ring:
    def __init__(self, own):
        self.size = lax.axis_size("mp_0")
        self.chunks = {0: own}
        self.done = 0

    def passed(self, array, hop):
        return lax.ppermute(
            array, "mp_0", [(i, (i + hop) % self.size) for i in range(self.size)]
        )

    def step(self, later=None):
        size, k = self.size, self.done + 1
        self.chunks[k] = self.passed(self.chunks[k - 1], 1)
        if k < size // 2:
            self.chunks[size - k] = self.passed(self.chunks[(size - k + 1) % size], -1)
        self.done = k
        if later is not None:
            both = (later, self.chunks[k], self.chunks[size - k])
            later, self.chunks[k], self.chunks[size - k] = lax.optimization_barrier(both)
        return later

    def all(self):
        return tuple(self.chunks[k] for k in range(self.size))


def per_device(grad_out, hidden_act, carried, prior_right):
    own = carried[0]
    act = hidden_act.T
    features = own.shape[1]
    rank = prior_right.shape[1]
    replicas = lax.axis_size(DP)
    rows = own.shape[0] // 2
    tokens = hidden_act.shape[0]

    proj = call(
        proj_kernel,
        of((lax.axis_size("mp_0"), grad_out.shape[0], 2 * rank), bf16),
        limit=63,
        in_specs=[whole, whole],
        out_specs=whole,
        name="proj",
    )(grad_out, prior_right.T)
    proj, passed_on = lax.optimization_barrier((proj, grad_out))
    left = product(own, jnp.concatenate(halves(prior_right), axis=1), 1, 0)
    proj, left = lax.optimization_barrier((sent(proj, "mp_0"), left))
    ring = Ring(passed_on)
    proj = ring.step(proj)
    other = swapped(proj)
    left = call(
        local_left_kernel,
        of((lax.axis_size("dp_0"), rows, 2 * rank), bf16),
        limit=24,
        in_specs=[whole] * 4,
        out_specs=whole,
        name="local_left",
    )(proj, other, left, act)
    left = call(
        row_sum_kernel,
        of((lax.axis_size("dp_1"), rows, 2 * rank), bf16),
        in_specs=[whole],
        out_specs=whole,
        name="row_sum",
    )(sent(left, "dp_0"))
    parts = sent(left, "dp_1")
    for _ in range(3):
        ring.step()
    chunks = ring.all()

    width = features // 4
    half = tokens // 2
    left, turned, gram, keep, give = call(
        left_kernel,
        (
            of((rows, 2 * rank), bf16),
            of((2 * rank, rows), bf16),
            of((rank // 2, 2 * rank), f32),
            of((half, 2 * rank), bf16),
            of((half, 2 * rank), bf16),
        ),
        limit=50,
        in_specs=[whole, in_hbm],
        out_specs=(in_hbm,) + (whole,) * 4,
        scratch_shapes=[
            VMEM(act.shape, bf16),
            VMEM((rows, 2 * rank), bf16),
            pltpu.SemaphoreType.DMA((2,)),
        ],
        name="left_sum",
    )(parts, act)
    right = call(
        own_kernel,
        of((rank, features), f32),
        limit=50,
        in_specs=[whole, in_hbm],
        out_specs=whole,
        scratch_shapes=[VMEM(own.shape, bf16), pltpu.SemaphoreType.DMA((4,))],
        name="own_product",
    )(turned, own)

    right, half_out = call(
        functools.partial(right_kernel, len(chunks)),
        (of((16, rank // 4, width), bf16), of((half, features), bf16)),
        limit=50,
        in_specs=[whole, whole, whole] + [anywhere] * len(chunks),
        out_specs=(whole, in_hbm),
        scratch_shapes=[VMEM((half, features), bf16), pltpu.SemaphoreType.DMA((2 * len(chunks),))],
        name="right_product",
    )(keep, swapped(give), right, *chunks)

    other_half = swapped(half_out)
    other_gram = swapped(gram)
    right = sent(right, DP)
    right, other_half, other_gram = lax.optimization_barrier((right, other_half, other_gram))
    columns = pl.BlockSpec((half, width), lambda j: (0, j))
    merged = call(
        merged_kernel,
        of(own.shape, bf16),
        limit=58,
        grid=(4,),
        in_specs=[
            pl.BlockSpec((2 * rows, tokens), lambda j: (0, 0)),
            pl.BlockSpec((2 * rows, width), lambda j: (0, j)),
            columns,
            columns,
        ],
        out_specs=pl.BlockSpec((2 * rows, width), lambda j: (0, j)),
        scratch_shapes=[VMEM((tokens, width), bf16)],
        name="merged",
    )(act, own, half_out, other_half)
    right = call(
        replica_sum_kernel,
        of((rank // 4, width), bf16),
        in_specs=[whole],
        out_specs=whole,
        name="replica_sum",
    )(right)
    right = call(
        core_sum_kernel,
        of((8, rank // 4, width + 384), bf16),
        in_specs=[whole] * 4,
        out_specs=whole,
        name="core_sum",
    )(right, swapped(right), gram, other_gram)
    right, merged = lax.optimization_barrier((sent(right, "mp_0"), merged))
    right, gram = call(
        chip_sum_kernel,
        (of((16, rank // 4, width), bf16), of((rank // 4, 2 * rank), f32)),
        in_specs=[whole],
        out_specs=(whole, whole),
        name="chip_sum",
    )(right)
    right = sent(right, DP)
    inverse, ortho = call(
        inverse_kernel,
        (of((rank, 3 * rank), bf16), of((2 * rows, 3 * rank), bf16)),
        in_specs=[whole] * 3,
        out_specs=(whole, whole),
        name="inverse",
    )(gram, swapped(gram), left)
    right = right.reshape(4, 4, rank // 4, width)

    residual_out, next_right = call(
        functools.partial(residual_kernel, replicas),
        (of(own.shape, bf16), of((rank, features), f32)),
        limit=52,
        grid=(4,),
        in_specs=[
            whole,
            whole,
            whole,
            pl.BlockSpec((2 * rows, width), lambda j: (0, j)),
        ],
        out_specs=(
            pl.BlockSpec((2 * rows, width), lambda j: (0, j)),
            pl.BlockSpec((rank, width), lambda j: (0, j)),
        ),
        name="residual",
    )(inverse, ortho, right, merged)
    return (residual_out[None], next_right.T)


def solution(mesh):
    parted = Mesh(mesh.devices.reshape(4, 4, 8, 2), DP_MP)
    placed = (P(DP_MP, None), P(DP, MP), P(DP, MP, None), P())
    return jax.shard_map(
        per_device, mesh=parted, in_specs=placed, out_specs=(P(DP, MP, None), P()), check_vma=False
    )
```
